32 devices in a mesh: clips: 2 (over y), tiles: 4 (over z), frames: 2 (over x), chan: 2 (over core).
Axes of the slice: x: 2, y: 2, z: 4, core: 2. Of those that a mesh axis runs over, the one named last changes fastest.
Arguments:
- lr_feats: bfloat16 [8, 2, 64, 32, 128], P('clips', 'frames', 'chan', 'tiles'), parts along dimension 0, may hold values from -6 to 6
- flow_prev: int32 [8, 2, 4, 2], P('clips', None, 'tiles'), parts along dimension 0, may hold values from -8 to 8, as said below
- flow_second: int32 [8, 2, 4, 2], P('clips', None, 'tiles'), parts along dimension 0, may hold values from -8 to 8, as said below
- w_join: bfloat16 [9, 64, 192], P(None, 'chan'), may hold values from -0.15625 to 0.15625
- b_join: float32 [64], P('chan'), may hold values from -3 to 3
- w_first: bfloat16 [1, 9, 64, 64], P(None, None, 'chan'), may hold values from -0.25 to 0.25
- b_first: float32 [1, 64], P(None, 'chan'), may hold values from -3 to 3
- w_second: bfloat16 [1, 9, 64, 64], P(None, None, 'chan'), may hold values from -0.25 to 0.25
- b_second: float32 [1, 64], P(None, 'chan'), may hold values from -3 to 3
Outputs:
- hidden: bfloat16 [8, 2, 64, 32, 128], P('clips', 'frames', 'chan', 'tiles'), parts along dimension 0
The draws below stay inside these ranges and needn't reach their ends.
There are 2 independent parts, one for each index of `clips`. The reference program is written for one: setup_inputs(seed, part) draws one part's arguments, and reference() takes and returns one part's arrays. A program takes and returns all parts, laid end to end along the dimension named above; an argument that names none is the same for every part. Nothing has to cross between parts.
Inputs may be any that keep to these rules, and one draw needn't show every extreme that they name: `flow_prev`: both entries (dy, dx) of every block lie in the range; +8 and -8 each occur in every draw. `flow_second`: both entries (dy, dx) of every block lie in the range; +8 and -8 each occur in every draw.
All inputs are finite; a program needn't handle non-finite values.
Results may differ from the reference program's by a relative error of at most 0.012.
Values may be sent and summed in bfloat16 or wider, within the bound.
A program may use at most 64 MiB of HBM per device.

```python
import jax
import jax.numpy as jnp
from jax import lax

C = 64
RES = 1
BH = 8
COLS = 128
TR = 8
SEGS = 4
FRAMES = 2
ROWS = 32
NBLK = 4


def draw_offsets(key, salt_value):
    inner_key = jax.random.fold_in(key, salt_value)
    key_first, key_second, key_third = jax.random.split(inner_key, 3)
    count_all = SEGS * FRAMES * NBLK
    values = jax.random.randint(key_first, (count_all, 2), -TR, TR + 1, dtype=jnp.int32)
    top_index = jax.random.randint(key_second, (), 0, count_all, dtype=jnp.int32)
    low_index = jax.random.randint(key_third, (), 0, count_all, dtype=jnp.int32)
    values = values.at[top_index, 0].set(TR)
    values = values.at[low_index, 1].set(-TR)
    return values.reshape(SEGS, FRAMES, NBLK, 2)


def draw_flow_prev(key, part):
    return draw_offsets(key, 11)


def draw_flow_second(key, part):
    return draw_offsets(key, 23)


def block_levels(own_key, dims, shards, smallest, largest):
    loudness, own = 1.0, jax.random.fold_in(own_key, 6)
    for position, parts in shards:
        heights = jnp.exp(jax.random.uniform(jax.random.fold_in(own, position), (parts,), jnp.float32, smallest / len(shards), largest / len(shards)))
        loudness = loudness * jnp.repeat(heights, dims[position] // parts).reshape([-1 if axis == position else 1 for axis in range(len(dims))])
    return loudness


def normal_values(rng, extent, deviation, bound, cuts=(), kind=jnp.bfloat16):
    result = jax.random.normal(rng, extent, jnp.float32) * deviation
    if len(cuts) > 0:
        result = block_levels(rng, extent, cuts, -0.22, 0.18) * result
    return jnp.clip(result, min=-bound, max=bound).astype(kind)


def setup_inputs(seed: int = 0, part: int = 0) -> dict:
    key_of = jax.random.split(jax.random.key(seed), 10)
    own_keys = jax.random.split(jax.random.fold_in(key_of[9], part), 10)
    lr_feats = normal_values(own_keys[0], (SEGS, FRAMES, C, ROWS, COLS), 1.0, 6.0, ((1, 2), (2, 2), (3, 4)))
    flow_prev = draw_flow_prev(jax.random.fold_in(jax.random.fold_in(key_of[9], part), 71), part)
    flow_second = draw_flow_second(jax.random.fold_in(jax.random.fold_in(key_of[9], part), 71), part)
    w_join = normal_values(key_of[3], (9, C, 3 * C), (27 * C) ** -0.5, 0.15625, ((1, 2),))
    b_join = normal_values(key_of[4], (C,), 0.5, 3.0, ((0, 2),), jnp.float32)
    w_first = normal_values(key_of[5], (RES, 9, C, C), (9 * C) ** -0.5, 0.25, ((2, 2),))
    b_first = normal_values(key_of[6], (RES, C), 0.5, 3.0, ((1, 2),), jnp.float32)
    w_second = normal_values(key_of[7], (RES, 9, C, C), (9 * C) ** -0.5, 0.25, ((2, 2),))
    b_second = normal_values(key_of[8], (RES, C), 0.5, 3.0, ((1, 2),), jnp.float32)
    return dict(lr_feats=lr_feats, flow_prev=flow_prev, flow_second=flow_second, w_join=w_join, b_join=b_join, w_first=w_first, b_first=b_first, w_second=w_second, b_second=b_second)


def shift_blocks(feature, offsets):
    channels = feature.shape[0]
    col_count = feature.shape[2]
    padded = jnp.pad(feature, ((0, 0), (TR, TR), (TR, TR)))

    def take_block(block_number):
        start_row = (TR + block_number * BH + offsets[block_number, 0]).astype(jnp.int32)
        start_col = (TR + offsets[block_number, 1]).astype(jnp.int32)
        return lax.dynamic_slice(padded, (jnp.zeros((), jnp.int32), start_row, start_col), (channels, BH, col_count))

    pieces = jax.vmap(take_block)(jnp.arange(NBLK, dtype=jnp.int32))
    return jnp.transpose(pieces, (1, 0, 2, 3)).reshape(channels, NBLK * BH, col_count)


def convolve(inputs, weights, bias_vec):
    in_count, row_count, col_count = inputs.shape
    padded = jnp.pad(inputs, ((0, 0), (1, 1), (1, 1)))
    total_sum = jnp.zeros((weights.shape[1], row_count * col_count), jnp.float32)
    for tap_index in range(9):
        tap_row = tap_index // 3
        tap_col = tap_index % 3
        window = padded[:, tap_row:tap_row + row_count, tap_col:tap_col + col_count].reshape(in_count, row_count * col_count)
        total_sum = total_sum + jnp.dot(weights[tap_index], window, preferred_element_type=jnp.float32)
    return total_sum.reshape(-1, row_count, col_count) + bias_vec[:, None, None]


def refine(current, warped_one, warped_two, w_join, b_join, w_first, b_first, w_second, b_second):
    stacked = jnp.concatenate([current, warped_one, warped_two], axis=0)
    joined_sum = convolve(stacked, w_join, b_join)
    joined_state = jnp.where(joined_sum > 0, joined_sum, 0.1 * joined_sum).astype(jnp.bfloat16)
    for block_index in range(RES):
        inner_act = jnp.maximum(convolve(joined_state, w_first[block_index], b_first[block_index]), 0.0).astype(jnp.bfloat16)
        joined_state = (joined_state.astype(jnp.float32) + convolve(inner_act, w_second[block_index], b_second[block_index])).astype(jnp.bfloat16)
    return joined_state


def reference(lr_feats, flow_prev, flow_second, w_join, b_join, w_first, b_first, w_second, b_second):
    zero_feat = jnp.zeros(lr_feats.shape[2:], lr_feats.dtype)
    all_segments = []
    for segment in range(SEGS):
        older_feat = zero_feat
        newer_feat = zero_feat
        frame_list = []
        for frame_index in range(FRAMES):
            warped_one = shift_blocks(newer_feat, flow_prev[segment, frame_index])
            warped_two = shift_blocks(older_feat, flow_second[segment, frame_index])
            fresh_state = refine(lr_feats[segment, frame_index], warped_one, warped_two, w_join, b_join, w_first, b_first, w_second, b_second)
            frame_list.append(fresh_state)
            older_feat = newer_feat
            newer_feat = fresh_state
        all_segments.append(jnp.stack(frame_list))
    return jnp.stack(all_segments)
```

```python
import functools

import jax
import jax.numpy as jnp
from jax import lax
from jax.experimental import pallas as pl
from jax.experimental.pallas import tpu as pltpu
from jax.sharding import PartitionSpec as P

BH = 8


def padded_2(array, sides, width):
    for axis, dim in sides:
        devices, length = (lax.axis_size(axis), array.shape[dim])
        up = [(i, (i + 1) % devices) for i in range(devices - 1)]
        down = [(j, i) for i, j in up]
        last = lax.slice_in_dim(array, length - width, length, axis=dim)
        first = lax.slice_in_dim(array, 0, width, axis=dim)
        before = lax.ppermute(last, axis, up)
        after = lax.ppermute(first, axis, down)
        array = jnp.concatenate([before, array, after], axis=dim)
    return array


def for_sending(array):
    return jax.tree.map(lambda a: a.astype(jnp.bfloat16) if a.dtype == jnp.float32 else a, array)


def shifted(block, axis, distance):
    devices = range(lax.axis_size(axis))
    route = [(i - distance, i) for i in devices if i - distance in devices]
    return lax.ppermute(block, axis, route)


def displace(rimmed, offsets, tile_rows):
    channels = rimmed.shape[0]
    col_count = rimmed.shape[2]
    padded = jnp.pad(rimmed, ((0, 0), (0, 0), (tile_rows, tile_rows)))
    start_row = tile_rows + offsets[0, 0]
    start_col = tile_rows + offsets[0, 1]
    pieces = [lax.dynamic_slice(padded, (0, start_row, start_col), (channels, BH, col_count))]
    return jnp.concatenate(pieces, axis=1)


def convolve_rows(inputs, weights, bias_vec):
    in_count, row_count, col_count = inputs.shape
    rimmed = padded_2(inputs, (("tiles", 1),), 1)
    padded = jnp.pad(rimmed, ((0, 0), (0, 0), (1, 1)))
    total_sum = jnp.zeros((weights.shape[1], row_count * col_count), jnp.float32)
    for tap_index in range(9):
        tap_row = tap_index // 3
        tap_col = tap_index % 3
        window = padded[:, tap_row : tap_row + row_count, tap_col : tap_col + col_count].reshape(
            in_count, row_count * col_count
        )
        total_sum = total_sum + jnp.dot(
            weights[tap_index], window, preferred_element_type=jnp.float32
        )
    return total_sum.reshape(-1, row_count, col_count) + bias_vec[:, None, None]


def block_conv(own_part, weights, bias_vec):
    whole_input = lax.all_gather(own_part, "chan", axis=0, tiled=True)
    return convolve_rows(whole_input, weights, bias_vec)


def refine(current, warped_one, warped_two, w_join, b_join, w_first, b_first, w_second, b_second):
    full_current, full_one, full_two = (
        lax.all_gather(current, "chan", axis=0, tiled=True),
        lax.all_gather(warped_one, "chan", axis=0, tiled=True),
        lax.all_gather(warped_two, "chan", axis=0, tiled=True),
    )
    stacked = jnp.concatenate([full_current, full_one, full_two], axis=0)
    joined_sum = convolve_rows(stacked, w_join, b_join)
    joined_state = jnp.where(joined_sum > 0, joined_sum, 0.1 * joined_sum).astype(jnp.bfloat16)
    inner_act = jnp.maximum(block_conv(joined_state, w_first[0], b_first[0]), 0.0).astype(
        jnp.bfloat16
    )
    joined_state = (
        joined_state.astype(jnp.float32) + block_conv(inner_act, w_second[0], b_second[0])
    ).astype(jnp.bfloat16)
    return joined_state


def shards(lr_feats, flow_prev, flow_second, w_join, b_join, w_first, b_first, w_second, b_second):
    segments = lr_feats.shape[0]
    tile_rows = lr_feats.shape[3]
    frames_all = flow_prev.shape[1]
    owners = lax.axis_size("frames")
    position = lax.axis_index("frames")
    blank_feat = jnp.zeros(lr_feats.shape[2:], lr_feats.dtype)

    def advance(turn_index, carried):
        results, first_in, second_in, second_wait = carried
        segment = turn_index - position
        is_valid = (segment >= 0) & (segment < segments)
        seg_clip = jnp.clip(segment, 0, segments - 1)
        current = lax.dynamic_index_in_dim(lr_feats, seg_clip, 0, keepdims=False)[0]
        fresh_state = refine(
            current, first_in, second_in, w_join, b_join, w_first, b_first, w_second, b_second
        )
        kept_slice = lax.dynamic_index_in_dim(results, seg_clip, 0, keepdims=True)
        chosen = jnp.where(is_valid, fresh_state[None, None], kept_slice)
        results = lax.dynamic_update_index_in_dim(results, chosen[0], seg_clip, 0)
        rimmed_own = padded_2(fresh_state, (("tiles", 1),), tile_rows)
        frame_next = jnp.minimum(position + 1, frames_all - 1)
        frame_after = jnp.minimum(position + 2, frames_all - 1)
        ahead_one = displace(rimmed_own, flow_prev[seg_clip, frame_next], tile_rows)
        ahead_two = displace(rimmed_own, flow_second[seg_clip, frame_after], tile_rows)
        first_next = shifted(for_sending(ahead_one), "frames", 1).astype(ahead_one.dtype)
        wait_next = shifted(for_sending(ahead_two), "frames", 2).astype(ahead_two.dtype)
        return (results, first_next, second_wait, wait_next)

    initial = (jnp.zeros_like(lr_feats), blank_feat, blank_feat, blank_feat)
    results, first_in, second_in, second_wait = lax.fori_loop(
        0, segments + owners - 1, advance, initial
    )
    return results


MESH = pl.DeviceIdType.MESH


def plain_kernel(
    sizes,
    lr_ref, fl_ref, wj_ref, w1_ref, w2_ref, bias_ref,
    out_ref,
    L, H, blank, FL, FS, WJ, W1, W2, B,
    lr_send, lr_recv, fl_send, fl_recv, fl_sem, w_send, w_recv, h_send, h_recv, o_send, o_recv,
):
    frames, chans, tiles, rows, half, cols, blocks = sizes
    halo = 1 + 2 * blocks
    reach = rows + halo
    full = half * chans
    clip = lax.axis_index("clips")
    z = lax.axis_index("tiles")
    x = lax.axis_index("frames")
    c = lax.axis_index("chan")
    shot = x * chans + c
    group = [(f, k) for f in range(frames) for k in range(chans)]

    def has(step):
        return (z + step >= 0) & (z + step < tiles)

    def not_me(f, k):
        return jnp.logical_not((x == f) & (c == k))

    def half_of(k):
        return pl.ds(k * half if isinstance(k, int) else pl.multiple_of(k * half, half), half)

    def remote(src, dst, send, recv, dev):
        return pltpu.make_async_remote_copy(
            src_ref=src, dst_ref=dst, send_sem=send, recv_sem=recv,
            device_id=(clip,) + dev, device_id_type=MESH,
        )

    for f in range(frames):
        for part in (slice(0, halo), slice(halo + rows, 2 * halo + rows)):
            L[f, part] = jnp.zeros((halo, full, cols), L.dtype)
        for part in (slice(0, reach), slice(reach + rows, 2 * reach + rows)):
            H[f, part] = jnp.zeros((reach, full, cols), H.dtype)
    FL[...] = jnp.zeros(FL.shape, FL.dtype)

    barrier = pltpu.get_barrier_semaphore()

    def greet(dev):
        pl.semaphore_signal(barrier, inc=1, device_id=(clip,) + dev, device_id_type=MESH)

    count = len(group) - 1
    for f, k in group:
        @pl.when(not_me(f, k))
        def _():
            greet((z, f, k))
    for step in (-1, 1):
        for f, k in group:
            @pl.when(has(step))
            def _():
                greet((z + step, f, k))
        count = count + jnp.where(has(step), len(group), 0)
    for step in (-2, 2):
        @pl.when(has(step))
        def _():
            greet((z + step, x, c))
        count = count + jnp.where(has(step), 1, 0)
    pl.semaphore_wait(barrier, count)

    span = {0: (0, rows, halo), 1: (rows - halo, halo, 0), -1: (0, halo, halo + rows)}

    def lr_copy(f, k, step, src_f, src_k):
        start, length, land = span[step]
        return remote(
            lr_ref.at[f * chans + k, pl.ds(start, length)],
            L.at[src_f, pl.ds(land, length), half_of(src_k)],
            lr_send.at[f, k, step + 1], lr_recv.at[src_f, src_k, step + 1],
            (z + step, f, k),
        )

    def w_copies(k, src_k):
        pairs = [(wj_ref, WJ.at[:, half_of(src_k)]), (w1_ref, W1.at[:, :, half_of(src_k)]),
                 (w2_ref, W2.at[:, :, half_of(src_k)]), (bias_ref, B.at[:, half_of(src_k)])]
        return [remote(a, b, w_send.at[k, n], w_recv.at[src_k, n], (z, x, k))
                for n, (a, b) in enumerate(pairs)]

    def fl_copy(step):
        return remote(fl_ref.at[shot], FL.at[1 - step], fl_send.at[step + 1],
                      fl_recv.at[step + 1], (z + step, x, c))

    for step in (0, -1, 1):
        for f, k in group:
            @pl.when(not_me(f, k) if step == 0 else has(step))
            def _():
                lr_copy(f, k, step, x, c).start()
    for k in range(chans):
        @pl.when(c != k)
        def _():
            for copy in w_copies(k, c):
                copy.start()
    for step in (-1, 1):
        @pl.when(has(step))
        def _():
            fl_copy(step).start()
    L[x, halo:halo + rows, half_of(c), :] = lr_ref[shot]
    WJ[:, half_of(c), :] = wj_ref[...]
    W1[:, :, half_of(c), :] = w1_ref[...]
    W2[:, :, half_of(c), :] = w2_ref[...]
    B[:, half_of(c), :] = bias_ref[...]
    FL[1] = fl_ref[shot]
    blank[...] = jnp.zeros(blank.shape, blank.dtype)
    for step in (-1, 1):
        @pl.when(has(-step))
        def _():
            fl_copy(step).wait_recv()
    to_scalars = pltpu.make_async_copy(FL, FS, fl_sem)
    to_scalars.start()
    to_scalars.wait()

    lane = lax.broadcasted_iota(jnp.int32, (full, cols), 1)

    def displaced(which, t):
        age = t - 1 - which
        rows_out = []
        for j in range(-halo, rows + halo):
            near = 0 if j < 0 else (1 if j < rows else 2)
            entry = (which * frames + t) * 2
            dy = FS[near, entry, 0]
            dx = FS[near, entry + 1, 0]
            source = reach + j + dy
            v = (H[age, source] if age >= 0 else blank[source]).astype(jnp.float32)
            turned = pltpu.roll(v, lax.rem(cols - dx, cols), 1)
            seen = lane + dx
            rows_out.append(
                jnp.where((seen >= 0) & (seen < cols), turned, 0.0).astype(jnp.bfloat16))
        return jnp.concatenate(rows_out, axis=1)

    def conv(weights, inputs, count, bias):
        y = jnp.dot(weights, inputs, preferred_element_type=jnp.float32)
        result = []
        for r in range(1, count - 1):
            sides = []
            for j in range(3):
                total = None
                for i in range(3):
                    first = (3 * i + j) * full
                    part = y[first:first + full, (r + i - 1) * cols:(r + i) * cols]
                    total = part if total is None else total + part
                sides.append(total)
            left = jnp.where(lane == 0, 0.0, pltpu.roll(sides[0], 1, 1))
            right = jnp.where(lane == cols - 1, 0.0, pltpu.roll(sides[2], cols - 1, 1))
            result.append(sides[1] + left + right + bias)
        return result

    def inside(values, first):
        kept = []
        for n, v in enumerate(values):
            j = first + n
            if j < 0:
                v = jnp.where(z > 0, v, 0.0)
            elif j >= rows:
                v = jnp.where(z < tiles - 1, v, 0.0)
            kept.append(v.astype(jnp.bfloat16))
        return kept

    def h_copy(t, step):
        start, length = (0, rows) if abs(step) == 1 else ((rows - halo, halo) if step > 0 else (0, halo))
        return remote(
            H.at[t, pl.ds(reach + start, length)],
            H.at[t, pl.ds(reach + start - step * rows, length)],
            h_send.at[t, step + 2], h_recv.at[t, step + 2], (z + step, x, c),
        )

    def o_copy(t, k, to_shot, src):
        return remote(H.at[t, pl.ds(reach, rows), half_of(k)], out_ref.at[to_shot],
                      o_send.at[t, k], o_recv.at[src], (z, t, k))

    for t in range(frames):
        warped_two = displaced(1, t)
        if t == 0:
            warped_one = displaced(0, t)
            for k in range(chans):
                @pl.when(c != k)
                def _():
                    for copy in w_copies(c, k):
                        copy.wait_recv()
        for k in range(chans):
            @pl.when(not_me(t, k))
            def _():
                lr_copy(x, c, 0, t, k).wait_recv()
            for step in (-1, 1):
                @pl.when(has(-step))
                def _():
                    lr_copy(x, c, step, t, k).wait_recv()
        if t > 0:
            for step in (-2, -1, 1, 2):
                @pl.when(has(-step))
                def _():
                    h_copy(t - 1, step).wait_recv()
            warped_one = displaced(0, t)
        current = jnp.concatenate([L[t, r] for r in range(rows + 2 * halo)], axis=1)
        stacked = jnp.concatenate([current, warped_one, warped_two], axis=0)
        edge = halo - 1
        joined = conv(WJ[...].reshape(9 * full, 3 * full), stacked, rows + 2 * halo, B[0])
        state = inside([jnp.maximum(v, 0.1 * v) for v in joined], -edge)
        for n in range(blocks):
            inner = conv(W1[n].reshape(9 * full, full), jnp.concatenate(state, axis=1),
                         rows + 2 * edge, B[1 + n])
            inner = inside([jnp.maximum(v, 0.0) for v in inner], 1 - edge)
            added = conv(W2[n].reshape(9 * full, full), jnp.concatenate(inner, axis=1),
                         rows + 2 * edge - 2, B[1 + blocks + n])
            state = inside([s.astype(jnp.float32) + v for s, v in zip(state[2:-2], added)],
                           2 - edge)
            edge -= 2
        for r in range(rows):
            H[t, reach + r] = state[r]
        if t < frames - 1:
            for step in (-1, 1, -2, 2):
                @pl.when(has(step))
                def _():
                    h_copy(t, step).start()
        for k in range(chans):
            @pl.when(not_me(t, k))
            def _():
                o_copy(t, k, shot, shot).start()

            @pl.when((x == t) & (c == k))
            def _():
                out_ref[shot] = H[t, reach:reach + rows, half_of(k), :]

    for f, k in group:
        @pl.when(not_me(f, k))
        def _():
            lr_copy(f, k, 0, x, c).wait_send()
            o_copy(0, 0, f * chans + k, f * chans + k).wait_recv()
        for step in (-1, 1):
            @pl.when(has(step))
            def _():
                lr_copy(f, k, step, x, c).wait_send()
    for k in range(chans):
        @pl.when(c != k)
        def _():
            for copy in w_copies(k, c):
                copy.wait_send()
    for step in (-1, 1):
        @pl.when(has(step))
        def _():
            fl_copy(step).wait_send()
    for t in range(frames):
        if t < frames - 1:
            for step in (-1, 1, -2, 2):
                @pl.when(has(step))
                def _():
                    h_copy(t, step).wait_send()
        for k in range(chans):
            @pl.when(not_me(t, k))
            def _():
                o_copy(t, k, shot, shot).wait_send()


def by_shots(lr_feats, flow_prev, flow_second, w_join, b_join, w_first, b_first, w_second, b_second):
    shots, _, half, rows, cols = lr_feats.shape
    frames = lax.axis_size("frames")
    chans = lax.axis_size("chan")
    tiles = lax.axis_size("tiles")
    blocks = w_first.shape[0]
    halo = 1 + 2 * blocks
    reach = rows + halo
    full = half * chans
    lr = jnp.swapaxes(lr_feats[:, 0], 1, 2)
    flows = jnp.stack([flow_prev[:, :, 0], flow_second[:, :, 0]], axis=1).reshape(shots, 4 * frames)
    flows = jnp.broadcast_to(flows[:, :, None], (shots, 4 * frames, 128))
    bias = jnp.concatenate([b_join[None], b_first, b_second], axis=0)
    bias = jnp.broadcast_to(bias[:, :, None], bias.shape + (cols,))
    kind = lr.dtype
    dma = pltpu.SemaphoreType.DMA
    out = pl.pallas_call(
        functools.partial(plain_kernel, (frames, chans, tiles, rows, half, cols, blocks)),
        out_shape=jax.ShapeDtypeStruct((shots, rows, half, cols), kind),
        in_specs=[pl.BlockSpec(memory_space=pltpu.VMEM)] * 6,
        out_specs=pl.BlockSpec(memory_space=pltpu.VMEM),
        scratch_shapes=[
            pltpu.VMEM((frames, rows + 2 * halo, full, cols), kind),
            pltpu.VMEM((frames, rows + 2 * reach, full, cols), kind),
            pltpu.VMEM((rows + 2 * reach, full, cols), kind),
            pltpu.VMEM((3, 4 * frames, 128), jnp.int32),
            pltpu.SMEM((3, 4 * frames, 128), jnp.int32),
            pltpu.VMEM((9, full, 3 * full), kind),
            pltpu.VMEM((blocks, 9, full, full), kind),
            pltpu.VMEM((blocks, 9, full, full), kind),
            pltpu.VMEM((1 + 2 * blocks, full, cols), jnp.float32),
            dma((frames, chans, 3)), dma((frames, chans, 3)), dma((3,)), dma((3,)), dma,
            dma((chans, 4)), dma((chans, 4)), dma((frames, 5)), dma((frames, 5)),
            dma((frames, chans)), dma((shots,)),
        ],
        compiler_params=pltpu.CompilerParams(
            collective_id=0, has_side_effects=True, vmem_limit_bytes=40 * 1024 * 1024
        ),
    )(lr, flows, w_join, w_first, w_second, bias)
    return jnp.swapaxes(out, 1, 2)[:, None]


def one_shot_each(lr_feats, flow_prev, flow_second, w_join, b_join, w_first, *rest):
    halo = 1 + 2 * w_first.shape[0]
    rows = lr_feats.shape[3]
    shots = lax.axis_size("frames") * lax.axis_size("chan")
    fits = (
        lr_feats.shape[0] == shots
        and flow_prev.shape[1] == lax.axis_size("frames")
        and flow_prev.shape[2] == 1
        and halo <= rows
        and lr_feats.shape[4] == 128
    )
    plan = by_shots if fits else shards
    return plan(lr_feats, flow_prev, flow_second, w_join, b_join, w_first, *rest)


def solution(mesh):
    in_specs = (
        P("clips", "frames", "chan", "tiles", None),
        P("clips", None, "tiles", None),
        P("clips", None, "tiles", None),
        P(None, "chan", None),
        P("chan"),
        P(None, None, "chan", None),
        P(None, "chan"),
        P(None, None, "chan", None),
        P(None, "chan"),
    )
    out_specs = P("clips", "frames", "chan", "tiles", None)
    return jax.shard_map(one_shot_each, mesh=mesh, in_specs=in_specs, out_specs=out_specs, check_vma=False)
```

```python
import functools

import jax
import jax.numpy as jnp
from jax import lax
from jax.experimental import pallas as pl
from jax.experimental.pallas import tpu as pltpu
from jax.sharding import PartitionSpec as P

BH = 8


def padded_2(array, sides, width):
    for axis, dim in sides:
        devices, length = (lax.axis_size(axis), array.shape[dim])
        up = [(i, (i + 1) % devices) for i in range(devices - 1)]
        down = [(j, i) for i, j in up]
        last = lax.slice_in_dim(array, length - width, length, axis=dim)
        first = lax.slice_in_dim(array, 0, width, axis=dim)
        before = lax.ppermute(last, axis, up)
        after = lax.ppermute(first, axis, down)
        array = jnp.concatenate([before, array, after], axis=dim)
    return array


def for_sending(array):
    return jax.tree.map(lambda a: a.astype(jnp.bfloat16) if a.dtype == jnp.float32 else a, array)


def shifted(block, axis, distance):
    devices = range(lax.axis_size(axis))
    route = [(i - distance, i) for i in devices if i - distance in devices]
    return lax.ppermute(block, axis, route)


def displace(rimmed, offsets, tile_rows):
    channels = rimmed.shape[0]
    col_count = rimmed.shape[2]
    padded = jnp.pad(rimmed, ((0, 0), (0, 0), (tile_rows, tile_rows)))
    start_row = tile_rows + offsets[0, 0]
    start_col = tile_rows + offsets[0, 1]
    pieces = [lax.dynamic_slice(padded, (0, start_row, start_col), (channels, BH, col_count))]
    return jnp.concatenate(pieces, axis=1)


def convolve_rows(inputs, weights, bias_vec):
    in_count, row_count, col_count = inputs.shape
    rimmed = padded_2(inputs, (("tiles", 1),), 1)
    padded = jnp.pad(rimmed, ((0, 0), (0, 0), (1, 1)))
    total_sum = jnp.zeros((weights.shape[1], row_count * col_count), jnp.float32)
    for tap_index in range(9):
        tap_row = tap_index // 3
        tap_col = tap_index % 3
        window = padded[:, tap_row : tap_row + row_count, tap_col : tap_col + col_count].reshape(
            in_count, row_count * col_count
        )
        total_sum = total_sum + jnp.dot(
            weights[tap_index], window, preferred_element_type=jnp.float32
        )
    return total_sum.reshape(-1, row_count, col_count) + bias_vec[:, None, None]


def block_conv(own_part, weights, bias_vec):
    whole_input = lax.all_gather(own_part, "chan", axis=0, tiled=True)
    return convolve_rows(whole_input, weights, bias_vec)


def refine(current, warped_one, warped_two, w_join, b_join, w_first, b_first, w_second, b_second):
    full_current, full_one, full_two = (
        lax.all_gather(current, "chan", axis=0, tiled=True),
        lax.all_gather(warped_one, "chan", axis=0, tiled=True),
        lax.all_gather(warped_two, "chan", axis=0, tiled=True),
    )
    stacked = jnp.concatenate([full_current, full_one, full_two], axis=0)
    joined_sum = convolve_rows(stacked, w_join, b_join)
    joined_state = jnp.where(joined_sum > 0, joined_sum, 0.1 * joined_sum).astype(jnp.bfloat16)
    inner_act = jnp.maximum(block_conv(joined_state, w_first[0], b_first[0]), 0.0).astype(
        jnp.bfloat16
    )
    joined_state = (
        joined_state.astype(jnp.float32) + block_conv(inner_act, w_second[0], b_second[0])
    ).astype(jnp.bfloat16)
    return joined_state


def shards(lr_feats, flow_prev, flow_second, w_join, b_join, w_first, b_first, w_second, b_second):
    segments = lr_feats.shape[0]
    tile_rows = lr_feats.shape[3]
    frames_all = flow_prev.shape[1]
    owners = lax.axis_size("frames")
    position = lax.axis_index("frames")
    blank_feat = jnp.zeros(lr_feats.shape[2:], lr_feats.dtype)

    def advance(turn_index, carried):
        results, first_in, second_in, second_wait = carried
        segment = turn_index - position
        is_valid = (segment >= 0) & (segment < segments)
        seg_clip = jnp.clip(segment, 0, segments - 1)
        current = lax.dynamic_index_in_dim(lr_feats, seg_clip, 0, keepdims=False)[0]
        fresh_state = refine(
            current, first_in, second_in, w_join, b_join, w_first, b_first, w_second, b_second
        )
        kept_slice = lax.dynamic_index_in_dim(results, seg_clip, 0, keepdims=True)
        chosen = jnp.where(is_valid, fresh_state[None, None], kept_slice)
        results = lax.dynamic_update_index_in_dim(results, chosen[0], seg_clip, 0)
        rimmed_own = padded_2(fresh_state, (("tiles", 1),), tile_rows)
        frame_next = jnp.minimum(position + 1, frames_all - 1)
        frame_after = jnp.minimum(position + 2, frames_all - 1)
        ahead_one = displace(rimmed_own, flow_prev[seg_clip, frame_next], tile_rows)
        ahead_two = displace(rimmed_own, flow_second[seg_clip, frame_after], tile_rows)
        first_next = shifted(for_sending(ahead_one), "frames", 1).astype(ahead_one.dtype)
        wait_next = shifted(for_sending(ahead_two), "frames", 2).astype(ahead_two.dtype)
        return (results, first_next, second_wait, wait_next)

    initial = (jnp.zeros_like(lr_feats), blank_feat, blank_feat, blank_feat)
    results, first_in, second_in, second_wait = lax.fori_loop(
        0, segments + owners - 1, advance, initial
    )
    return results


MESH = pl.DeviceIdType.MESH


def plain_kernel(
    sizes,
    lr_ref, fp_ref, fs_ref, wj_ref, w1_ref, w2_ref, bj_ref, b1_ref, b2_ref,
    out_ref,
    L, H, blank, FA, FL, FS, WJ, W1, W2, BA, B,
    lr_send, lr_recv, fl_send, fl_recv, fl_sem, w_send, w_recv, h_send, h_recv, o_send, o_recv,
):
    frames, chans, tiles, rows, half, cols, blocks = sizes
    halo = 1 + 2 * blocks
    reach = rows + halo
    full = half * chans
    clip = lax.axis_index("clips")
    z = lax.axis_index("tiles")
    x = lax.axis_index("frames")
    c = lax.axis_index("chan")
    shot = x * chans + c
    group = [(f, k) for f in range(frames) for k in range(chans)]

    def has(step):
        return (z + step >= 0) & (z + step < tiles)

    def not_me(f, k):
        return jnp.logical_not((x == f) & (c == k))

    def half_of(k):
        return pl.ds(k * half if isinstance(k, int) else pl.multiple_of(k * half, half), half)

    def remote(src, dst, send, recv, dev):
        return pltpu.make_async_remote_copy(
            src_ref=src, dst_ref=dst, send_sem=send, recv_sem=recv,
            device_id=(clip,) + dev, device_id_type=MESH,
        )

    for f in range(frames):
        for part in (slice(0, halo), slice(halo + rows, 2 * halo + rows)):
            L[f, part] = jnp.zeros((halo, full, cols), L.dtype)
        for part in (slice(0, reach), slice(reach + rows, 2 * reach + rows)):
            H[f, part] = jnp.zeros((reach, full, cols), H.dtype)
    FL[...] = jnp.zeros(FL.shape, FL.dtype)
    FA[...] = jnp.zeros(FA.shape, FA.dtype)
    BA[...] = jnp.zeros(BA.shape, BA.dtype)
    FA[0, :, 0:frames * chans] = fp_ref[...]
    FA[1, :, 0:frames * chans] = fs_ref[...]
    for n, ref in enumerate([bj_ref] + [b1_ref.at[m:m + 1] for m in range(blocks)] + [b2_ref.at[m:m + 1] for m in range(blocks)]):
        BA[n:n + 1, 0:half] = ref[...]

    barrier = pltpu.get_barrier_semaphore()

    def greet(dev):
        pl.semaphore_signal(barrier, inc=1, device_id=(clip,) + dev, device_id_type=MESH)

    count = len(group) - 1
    for f, k in group:
        @pl.when(not_me(f, k))
        def _():
            greet((z, f, k))
    for step in (-1, 1):
        for f, k in group:
            @pl.when(has(step))
            def _():
                greet((z + step, f, k))
        count = count + jnp.where(has(step), len(group), 0)
    for step in (-2, 2):
        @pl.when(has(step))
        def _():
            greet((z + step, x, c))
        count = count + jnp.where(has(step), 1, 0)
    pl.semaphore_wait(barrier, count)

    span = {0: (0, rows, halo), 1: (rows - halo, halo, 0), -1: (0, halo, halo + rows)}

    def lr_copy(f, k, step, src_f, src_k):
        start, length, land = span[step]
        return remote(
            lr_ref.at[f * chans + k, pl.ds(start, length)],
            L.at[src_f, pl.ds(land, length), half_of(src_k)],
            lr_send.at[f, k, step + 1], lr_recv.at[src_f, src_k, step + 1],
            (z + step, f, k),
        )

    def w_copies(k, src_k):
        pairs = [(wj_ref, WJ.at[:, half_of(src_k)]), (w1_ref, W1.at[:, :, half_of(src_k)]),
                 (w2_ref, W2.at[:, :, half_of(src_k)]), (BA, B.at[src_k])]
        return [remote(a, b, w_send.at[k, n], w_recv.at[src_k, n], (z, x, k))
                for n, (a, b) in enumerate(pairs)]

    def fl_copy(step):
        return remote(FA, FL.at[1 - step], fl_send.at[step + 1],
                      fl_recv.at[step + 1], (z + step, x, c))

    def send_lr(f, k, step):
        @pl.when(not_me(f, k) if step == 0 else has(step))
        def _():
            lr_copy(f, k, step, x, c).start()

    for step in (-1, 1):
        @pl.when(has(step))
        def _():
            fl_copy(step).start()
    for turn in range(frames):
        f = lax.rem(x + turn, frames)
        for step in (0, -1, 1):
            for k in range(chans):
                send_lr(f, k, step)
        if turn == 0:
            for k in range(chans):
                @pl.when(c != k)
                def _():
                    for copy in w_copies(k, c):
                        copy.start()
    L[x, halo:halo + rows, half_of(c), :] = lr_ref[shot]
    WJ[:, half_of(c), :] = wj_ref[...]
    W1[:, :, half_of(c), :] = w1_ref[...]
    W2[:, :, half_of(c), :] = w2_ref[...]
    B[c] = BA[...]
    FL[1] = FA[...]
    blank[...] = jnp.zeros(blank.shape, blank.dtype)
    for step in (-1, 1):
        @pl.when(has(-step))
        def _():
            fl_copy(step).wait_recv()
    to_scalars = pltpu.make_async_copy(FL, FS, fl_sem)
    to_scalars.start()
    to_scalars.wait()

    lane = lax.broadcasted_iota(jnp.int32, (full, cols), 1)

    def displaced(which, t):
        age = t - 1 - which
        rows_out = []
        for j in range(-halo, rows + halo):
            near = 0 if j < 0 else (1 if j < rows else 2)
            dy = FS[near, which, 2 * t, shot]
            dx = FS[near, which, 2 * t + 1, shot]
            source = reach + j + dy
            v = (H[age, source] if age >= 0 else blank[source]).astype(jnp.float32)
            turned = pltpu.roll(v, lax.rem(cols - dx, cols), 1)
            seen = lane + dx
            rows_out.append(
                jnp.where((seen >= 0) & (seen < cols), turned, 0.0).astype(jnp.bfloat16))
        return jnp.concatenate(rows_out, axis=1)

    def conv(weights, inputs, count, bias):
        y = jnp.dot(weights, inputs, preferred_element_type=jnp.float32)
        result = []
        for r in range(1, count - 1):
            sides = []
            for j in range(3):
                total = None
                for i in range(3):
                    first = (3 * i + j) * full
                    part = y[first:first + full, (r + i - 1) * cols:(r + i) * cols]
                    total = part if total is None else total + part
                sides.append(total)
            left = jnp.where(lane == 0, 0.0, pltpu.roll(sides[0], 1, 1))
            right = jnp.where(lane == cols - 1, 0.0, pltpu.roll(sides[2], cols - 1, 1))
            result.append(sides[1] + left + right + bias)
        return result

    def inside(values, first):
        kept = []
        for n, v in enumerate(values):
            j = first + n
            if j < 0:
                v = jnp.where(z > 0, v, 0.0)
            elif j >= rows:
                v = jnp.where(z < tiles - 1, v, 0.0)
            kept.append(v.astype(jnp.bfloat16))
        return kept

    def h_copy(t, step):
        start, length = (0, rows) if abs(step) == 1 else ((rows - halo, halo) if step > 0 else (0, halo))
        return remote(
            H.at[t, pl.ds(reach + start, length)],
            H.at[t, pl.ds(reach + start - step * rows, length)],
            h_send.at[t, step + 2], h_recv.at[t, step + 2], (z + step, x, c),
        )

    def o_copy(t, k, to_shot, src):
        return remote(H.at[t, pl.ds(reach, rows), half_of(k)], out_ref.at[to_shot],
                      o_send.at[t, k], o_recv.at[src], (z, t, k))

    corner = lax.broadcasted_iota(jnp.int32, (half, 128), 0) == lax.broadcasted_iota(
        jnp.int32, (half, 128), 1)

    def bias_of(n):
        parts = [jnp.sum(jnp.where(corner, B[k, n:n + 1, :], 0.0), axis=1, keepdims=True)
                 for k in range(chans)]
        return jnp.broadcast_to(jnp.concatenate(parts, axis=0), (full, cols))

    for t in range(frames):
        warped_two = displaced(1, t)
        if t == 0:
            warped_one = displaced(0, t)
            for k in range(chans):
                @pl.when(c != k)
                def _():
                    for copy in w_copies(c, k):
                        copy.wait_recv()
            biases = [bias_of(n) for n in range(1 + 2 * blocks)]
        for k in range(chans):
            @pl.when(not_me(t, k))
            def _():
                lr_copy(x, c, 0, t, k).wait_recv()
            for step in (-1, 1):
                @pl.when(has(-step))
                def _():
                    lr_copy(x, c, step, t, k).wait_recv()
        if t > 0:
            for step in (-2, -1, 1, 2):
                @pl.when(has(-step))
                def _():
                    h_copy(t - 1, step).wait_recv()
            warped_one = displaced(0, t)
        current = jnp.concatenate([L[t, r] for r in range(rows + 2 * halo)], axis=1)
        stacked = jnp.concatenate([current, warped_one, warped_two], axis=0)
        edge = halo - 1
        joined = conv(WJ[...].reshape(9 * full, 3 * full), stacked, rows + 2 * halo, biases[0])
        state = inside([jnp.maximum(v, 0.1 * v) for v in joined], -edge)
        for n in range(blocks):
            inner = conv(W1[n].reshape(9 * full, full), jnp.concatenate(state, axis=1),
                         rows + 2 * edge, biases[1 + n])
            inner = inside([jnp.maximum(v, 0.0) for v in inner], 1 - edge)
            added = conv(W2[n].reshape(9 * full, full), jnp.concatenate(inner, axis=1),
                         rows + 2 * edge - 2, biases[1 + blocks + n])
            state = inside([s.astype(jnp.float32) + v for s, v in zip(state[2:-2], added)],
                           2 - edge)
            edge -= 2
        for r in range(rows):
            H[t, reach + r] = state[r]
        if t < frames - 1:
            for step in (-1, 1, -2, 2):
                @pl.when(has(step))
                def _():
                    h_copy(t, step).start()
        for k in range(chans):
            @pl.when(not_me(t, k))
            def _():
                o_copy(t, k, shot, shot).start()

            @pl.when((x == t) & (c == k))
            def _():
                out_ref[shot] = H[t, reach:reach + rows, half_of(k), :]

    for f, k in group:
        @pl.when(not_me(f, k))
        def _():
            lr_copy(f, k, 0, x, c).wait_send()
            o_copy(0, 0, f * chans + k, f * chans + k).wait_recv()
        for step in (-1, 1):
            @pl.when(has(step))
            def _():
                lr_copy(f, k, step, x, c).wait_send()
    for k in range(chans):
        @pl.when(c != k)
        def _():
            for copy in w_copies(k, c):
                copy.wait_send()
    for step in (-1, 1):
        @pl.when(has(step))
        def _():
            fl_copy(step).wait_send()
    for t in range(frames):
        if t < frames - 1:
            for step in (-1, 1, -2, 2):
                @pl.when(has(step))
                def _():
                    h_copy(t, step).wait_send()
        for k in range(chans):
            @pl.when(not_me(t, k))
            def _():
                o_copy(t, k, shot, shot).wait_send()


def by_shots(lr_feats, flow_prev, flow_second, w_join, b_join, w_first, b_first, w_second, b_second):
    shots, _, half, rows, cols = lr_feats.shape
    frames = lax.axis_size("frames")
    chans = lax.axis_size("chan")
    tiles = lax.axis_size("tiles")
    blocks = w_first.shape[0]
    halo = 1 + 2 * blocks
    reach = rows + halo
    full = half * chans
    lr = jnp.swapaxes(lr_feats[:, 0], 1, 2)
    offsets = [jnp.transpose(f[:, :, 0], (1, 2, 0)).reshape(2 * frames, shots) for f in (flow_prev, flow_second)]
    lines = -(-(1 + 2 * blocks) // 8) * 8
    kind = lr.dtype
    dma = pltpu.SemaphoreType.DMA
    out = pl.pallas_call(
        functools.partial(plain_kernel, (frames, chans, tiles, rows, half, cols, blocks)),
        out_shape=jax.ShapeDtypeStruct((shots, rows, half, cols), kind),
        in_specs=[pl.BlockSpec(memory_space=pltpu.VMEM)] * 9,
        out_specs=pl.BlockSpec(memory_space=pltpu.VMEM),
        scratch_shapes=[
            pltpu.VMEM((frames, rows + 2 * halo, full, cols), kind),
            pltpu.VMEM((frames, rows + 2 * reach, full, cols), kind),
            pltpu.VMEM((rows + 2 * reach, full, cols), kind),
            pltpu.VMEM((2, 2 * frames, 128), jnp.int32),
            pltpu.VMEM((3, 2, 2 * frames, 128), jnp.int32),
            pltpu.SMEM((3, 2, 2 * frames, 128), jnp.int32),
            pltpu.VMEM((9, full, 3 * full), kind),
            pltpu.VMEM((blocks, 9, full, full), kind),
            pltpu.VMEM((blocks, 9, full, full), kind),
            pltpu.VMEM((lines, 128), jnp.float32),
            pltpu.VMEM((chans, lines, 128), jnp.float32),
            dma((frames, chans, 3)), dma((frames, chans, 3)), dma((3,)), dma((3,)), dma,
            dma((chans, 4)), dma((chans, 4)), dma((frames, 5)), dma((frames, 5)),
            dma((frames, chans)), dma((shots,)),
        ],
        compiler_params=pltpu.CompilerParams(
            collective_id=0, has_side_effects=True, vmem_limit_bytes=40 * 1024 * 1024
        ),
    )(lr, *offsets, w_join, w_first, w_second, b_join[None], b_first, b_second)
    return jnp.swapaxes(out, 1, 2)[:, None]


def one_shot_each(lr_feats, flow_prev, flow_second, w_join, b_join, w_first, *rest):
    halo = 1 + 2 * w_first.shape[0]
    rows = lr_feats.shape[3]
    shots = lax.axis_size("frames") * lax.axis_size("chan")
    fits = (
        lr_feats.shape[0] == shots
        and flow_prev.shape[1] == lax.axis_size("frames")
        and flow_prev.shape[2] == 1
        and halo <= rows
        and lr_feats.shape[4] == 128
        and lr_feats.shape[2] <= 128
        and lr_feats.shape[0] <= 128
    )
    plan = by_shots if fits else shards
    return plan(lr_feats, flow_prev, flow_second, w_join, b_join, w_first, *rest)


def solution(mesh):
    in_specs = (
        P("clips", "frames", "chan", "tiles", None),
        P("clips", None, "tiles", None),
        P("clips", None, "tiles", None),
        P(None, "chan", None),
        P("chan"),
        P(None, None, "chan", None),
        P(None, "chan"),
        P(None, None, "chan", None),
        P(None, "chan"),
    )
    out_specs = P("clips", "frames", "chan", "tiles", None)
    return jax.shard_map(one_shot_each, mesh=mesh, in_specs=in_specs, out_specs=out_specs, check_vma=False)
```

```python
import functools

import jax
import jax.numpy as jnp
from jax import lax
from jax.experimental import pallas as pl
from jax.experimental.pallas import tpu as pltpu
from jax.sharding import PartitionSpec as P

BH = 8


def padded_2(array, sides, width):
    for axis, dim in sides:
        devices, length = (lax.axis_size(axis), array.shape[dim])
        up = [(i, (i + 1) % devices) for i in range(devices - 1)]
        down = [(j, i) for i, j in up]
        last = lax.slice_in_dim(array, length - width, length, axis=dim)
        first = lax.slice_in_dim(array, 0, width, axis=dim)
        before = lax.ppermute(last, axis, up)
        after = lax.ppermute(first, axis, down)
        array = jnp.concatenate([before, array, after], axis=dim)
    return array


def for_sending(array):
    return jax.tree.map(lambda a: a.astype(jnp.bfloat16) if a.dtype == jnp.float32 else a, array)


def shifted(block, axis, distance):
    devices = range(lax.axis_size(axis))
    route = [(i - distance, i) for i in devices if i - distance in devices]
    return lax.ppermute(block, axis, route)


def displace(rimmed, offsets, tile_rows):
    channels = rimmed.shape[0]
    col_count = rimmed.shape[2]
    padded = jnp.pad(rimmed, ((0, 0), (0, 0), (tile_rows, tile_rows)))
    start_row = tile_rows + offsets[0, 0]
    start_col = tile_rows + offsets[0, 1]
    pieces = [lax.dynamic_slice(padded, (0, start_row, start_col), (channels, BH, col_count))]
    return jnp.concatenate(pieces, axis=1)


def convolve_rows(inputs, weights, bias_vec):
    in_count, row_count, col_count = inputs.shape
    rimmed = padded_2(inputs, (("tiles", 1),), 1)
    padded = jnp.pad(rimmed, ((0, 0), (0, 0), (1, 1)))
    total_sum = jnp.zeros((weights.shape[1], row_count * col_count), jnp.float32)
    for tap_index in range(9):
        tap_row = tap_index // 3
        tap_col = tap_index % 3
        window = padded[:, tap_row : tap_row + row_count, tap_col : tap_col + col_count].reshape(
            in_count, row_count * col_count
        )
        total_sum = total_sum + jnp.dot(
            weights[tap_index], window, preferred_element_type=jnp.float32
        )
    return total_sum.reshape(-1, row_count, col_count) + bias_vec[:, None, None]


def block_conv(own_part, weights, bias_vec):
    whole_input = lax.all_gather(own_part, "chan", axis=0, tiled=True)
    return convolve_rows(whole_input, weights, bias_vec)


def refine(current, warped_one, warped_two, w_join, b_join, w_first, b_first, w_second, b_second):
    full_current, full_one, full_two = (
        lax.all_gather(current, "chan", axis=0, tiled=True),
        lax.all_gather(warped_one, "chan", axis=0, tiled=True),
        lax.all_gather(warped_two, "chan", axis=0, tiled=True),
    )
    stacked = jnp.concatenate([full_current, full_one, full_two], axis=0)
    joined_sum = convolve_rows(stacked, w_join, b_join)
    joined_state = jnp.where(joined_sum > 0, joined_sum, 0.1 * joined_sum).astype(jnp.bfloat16)
    inner_act = jnp.maximum(block_conv(joined_state, w_first[0], b_first[0]), 0.0).astype(
        jnp.bfloat16
    )
    joined_state = (
        joined_state.astype(jnp.float32) + block_conv(inner_act, w_second[0], b_second[0])
    ).astype(jnp.bfloat16)
    return joined_state


def shards(lr_feats, flow_prev, flow_second, w_join, b_join, w_first, b_first, w_second, b_second):
    segments = lr_feats.shape[0]
    tile_rows = lr_feats.shape[3]
    frames_all = flow_prev.shape[1]
    owners = lax.axis_size("frames")
    position = lax.axis_index("frames")
    blank_feat = jnp.zeros(lr_feats.shape[2:], lr_feats.dtype)

    def advance(turn_index, carried):
        results, first_in, second_in, second_wait = carried
        segment = turn_index - position
        is_valid = (segment >= 0) & (segment < segments)
        seg_clip = jnp.clip(segment, 0, segments - 1)
        current = lax.dynamic_index_in_dim(lr_feats, seg_clip, 0, keepdims=False)[0]
        fresh_state = refine(
            current, first_in, second_in, w_join, b_join, w_first, b_first, w_second, b_second
        )
        kept_slice = lax.dynamic_index_in_dim(results, seg_clip, 0, keepdims=True)
        chosen = jnp.where(is_valid, fresh_state[None, None], kept_slice)
        results = lax.dynamic_update_index_in_dim(results, chosen[0], seg_clip, 0)
        rimmed_own = padded_2(fresh_state, (("tiles", 1),), tile_rows)
        frame_next = jnp.minimum(position + 1, frames_all - 1)
        frame_after = jnp.minimum(position + 2, frames_all - 1)
        ahead_one = displace(rimmed_own, flow_prev[seg_clip, frame_next], tile_rows)
        ahead_two = displace(rimmed_own, flow_second[seg_clip, frame_after], tile_rows)
        first_next = shifted(for_sending(ahead_one), "frames", 1).astype(ahead_one.dtype)
        wait_next = shifted(for_sending(ahead_two), "frames", 2).astype(ahead_two.dtype)
        return (results, first_next, second_wait, wait_next)

    initial = (jnp.zeros_like(lr_feats), blank_feat, blank_feat, blank_feat)
    results, first_in, second_in, second_wait = lax.fori_loop(
        0, segments + owners - 1, advance, initial
    )
    return results


MESH = pl.DeviceIdType.MESH


def plain_kernel(
    sizes,
    lr_ref, fp_ref, fs_ref, wj_ref, w1_ref, w2_ref, bj_ref, b1_ref, b2_ref,
    out_ref,
    L, H, blank, FA, FL, FS, WJ, W1, W2, BA, B,
    lr_send, lr_recv, fl_send, fl_recv, fl_sem, w_send, w_recv, h_send, h_recv, o_send, o_recv,
):
    frames, chans, tiles, rows, half, cols, blocks = sizes
    halo = 1 + 2 * blocks
    reach = rows + halo
    full = half * chans
    clip = lax.axis_index("clips")
    z = lax.axis_index("tiles")
    x = lax.axis_index("frames")
    c = lax.axis_index("chan")
    shot = x * chans + c
    group = [(f, k) for f in range(frames) for k in range(chans)]

    def has(step):
        return (z + step >= 0) & (z + step < tiles)

    def not_me(f, k):
        return jnp.logical_not((x == f) & (c == k))

    def half_of(k):
        return pl.ds(k * half if isinstance(k, int) else pl.multiple_of(k * half, half), half)

    def remote(src, dst, send, recv, dev):
        return pltpu.make_async_remote_copy(
            src_ref=src, dst_ref=dst, send_sem=send, recv_sem=recv,
            device_id=(clip,) + dev, device_id_type=MESH,
        )

    for f in range(frames):
        for part in (slice(0, halo), slice(halo + rows, 2 * halo + rows)):
            L[f, part] = jnp.zeros((halo, full, cols), L.dtype)
        for part in (slice(0, reach), slice(reach + rows, 2 * reach + rows)):
            H[f, part] = jnp.zeros((reach, full, cols), H.dtype)
    FL[...] = jnp.zeros(FL.shape, FL.dtype)
    FA[...] = jnp.zeros(FA.shape, FA.dtype)
    BA[...] = jnp.zeros(BA.shape, BA.dtype)
    FA[0, :, 0:frames * chans] = fp_ref[...]
    FA[1, :, 0:frames * chans] = fs_ref[...]
    for n, ref in enumerate([bj_ref] + [b1_ref.at[m:m + 1] for m in range(blocks)] + [b2_ref.at[m:m + 1] for m in range(blocks)]):
        BA[n:n + 1, 0:half] = ref[...]

    barrier = pltpu.get_barrier_semaphore()

    def greet(dev):
        pl.semaphore_signal(barrier, inc=1, device_id=(clip,) + dev, device_id_type=MESH)

    count = len(group) - 1
    for f, k in group:
        @pl.when(not_me(f, k))
        def _():
            greet((z, f, k))
    for step in (-1, 1):
        for f, k in group:
            @pl.when(has(step))
            def _():
                greet((z + step, f, k))
        count = count + jnp.where(has(step), len(group), 0)
    for step in (-2, 2):
        @pl.when(has(step))
        def _():
            greet((z + step, x, c))
        count = count + jnp.where(has(step), 1, 0)
    pl.semaphore_wait(barrier, count)

    span = {0: (0, rows, halo), 1: (rows - halo, halo, 0), -1: (0, halo, halo + rows)}

    def lr_copy(f, k, step, src_f, src_k):
        start, length, land = span[step]
        return remote(
            lr_ref.at[f * chans + k, pl.ds(start, length)],
            L.at[src_f, pl.ds(land, length), half_of(src_k)],
            lr_send.at[f, k, step + 1], lr_recv.at[src_f, src_k, step + 1],
            (z + step, f, k),
        )

    def w_copies(k, src_k):
        pairs = [(wj_ref, WJ.at[:, half_of(src_k)]), (w1_ref, W1.at[:, :, half_of(src_k)]),
                 (w2_ref, W2.at[:, :, half_of(src_k)]), (BA, B.at[src_k])]
        return [remote(a, b, w_send.at[k, n], w_recv.at[src_k, n], (z, x, k))
                for n, (a, b) in enumerate(pairs)]

    def fl_copy(step):
        return remote(FA, FL.at[1 - step], fl_send.at[step + 1],
                      fl_recv.at[step + 1], (z + step, x, c))

    def send_lr(f, k, step):
        @pl.when(not_me(f, k) if step == 0 else has(step))
        def _():
            lr_copy(f, k, step, x, c).start()

    for step in (-1, 1):
        @pl.when(has(step))
        def _():
            fl_copy(step).start()
    for step in (0, -1, 1):
        for turn in range(frames):
            f = lax.rem(x + frames - 1 - turn, frames)
            for k in range(chans):
                send_lr(f, k, step)
        if step == 0:
            for k in range(chans):
                @pl.when(c != k)
                def _():
                    for copy in w_copies(k, c):
                        copy.start()
    L[x, halo:halo + rows, half_of(c), :] = lr_ref[shot]
    WJ[:, half_of(c), :] = wj_ref[...]
    W1[:, :, half_of(c), :] = w1_ref[...]
    W2[:, :, half_of(c), :] = w2_ref[...]
    B[c] = BA[...]
    FL[1] = FA[...]
    blank[...] = jnp.zeros(blank.shape, blank.dtype)
    for step in (-1, 1):
        @pl.when(has(-step))
        def _():
            fl_copy(step).wait_recv()
    to_scalars = pltpu.make_async_copy(FL, FS, fl_sem)
    to_scalars.start()
    to_scalars.wait()

    lane = lax.broadcasted_iota(jnp.int32, (full, cols), 1)

    def displaced(which, t):
        age = t - 1 - which
        rows_out = []
        for j in range(-halo, rows + halo):
            near = 0 if j < 0 else (1 if j < rows else 2)
            dy = FS[near, which, 2 * t, shot]
            dx = FS[near, which, 2 * t + 1, shot]
            source = reach + j + dy
            v = (H[age, source] if age >= 0 else blank[source]).astype(jnp.float32)
            turned = pltpu.roll(v, lax.rem(cols - dx, cols), 1)
            seen = lane + dx
            rows_out.append(
                jnp.where((seen >= 0) & (seen < cols), turned, 0.0).astype(jnp.bfloat16))
        return jnp.concatenate(rows_out, axis=1)

    def conv(weights, inputs, count, bias):
        y = jnp.dot(weights, inputs, preferred_element_type=jnp.float32)
        result = []
        for r in range(1, count - 1):
            sides = []
            for j in range(3):
                total = None
                for i in range(3):
                    first = (3 * i + j) * full
                    part = y[first:first + full, (r + i - 1) * cols:(r + i) * cols]
                    total = part if total is None else total + part
                sides.append(total)
            left = jnp.where(lane == 0, 0.0, pltpu.roll(sides[0], 1, 1))
            right = jnp.where(lane == cols - 1, 0.0, pltpu.roll(sides[2], cols - 1, 1))
            result.append(sides[1] + left + right + bias)
        return result

    def inside(values, first):
        kept = []
        for n, v in enumerate(values):
            j = first + n
            if j < 0:
                v = jnp.where(z > 0, v, 0.0)
            elif j >= rows:
                v = jnp.where(z < tiles - 1, v, 0.0)
            kept.append(v.astype(jnp.bfloat16))
        return kept

    def h_copy(t, step):
        start, length = (0, rows) if abs(step) == 1 else ((rows - halo, halo) if step > 0 else (0, halo))
        return remote(
            H.at[t, pl.ds(reach + start, length)],
            H.at[t, pl.ds(reach + start - step * rows, length)],
            h_send.at[t, step + 2], h_recv.at[t, step + 2], (z + step, x, c),
        )

    def o_copy(t, k, to_shot, src):
        return remote(H.at[t, pl.ds(reach, rows), half_of(k)], out_ref.at[to_shot],
                      o_send.at[t, k], o_recv.at[src], (z, t, k))

    corner = lax.broadcasted_iota(jnp.int32, (half, 128), 0) == lax.broadcasted_iota(
        jnp.int32, (half, 128), 1)

    def bias_of(n):
        parts = [jnp.sum(jnp.where(corner, B[k, n:n + 1, :], 0.0), axis=1, keepdims=True)
                 for k in range(chans)]
        return jnp.broadcast_to(jnp.concatenate(parts, axis=0), (full, cols))

    for t in range(frames):
        warped_two = displaced(1, t)
        if t == 0:
            warped_one = displaced(0, t)
            for k in range(chans):
                @pl.when(c != k)
                def _():
                    for copy in w_copies(c, k):
                        copy.wait_recv()
            biases = [bias_of(n) for n in range(1 + 2 * blocks)]
        for k in range(chans):
            @pl.when(not_me(t, k))
            def _():
                lr_copy(x, c, 0, t, k).wait_recv()
            for step in (-1, 1):
                @pl.when(has(-step))
                def _():
                    lr_copy(x, c, step, t, k).wait_recv()
        if t > 0:
            for step in (-2, -1, 1, 2):
                @pl.when(has(-step))
                def _():
                    h_copy(t - 1, step).wait_recv()
            warped_one = displaced(0, t)
        current = jnp.concatenate([L[t, r] for r in range(rows + 2 * halo)], axis=1)
        stacked = jnp.concatenate([current, warped_one, warped_two], axis=0)
        edge = halo - 1
        joined = conv(WJ[...].reshape(9 * full, 3 * full), stacked, rows + 2 * halo, biases[0])
        state = inside([jnp.maximum(v, 0.1 * v) for v in joined], -edge)
        for n in range(blocks):
            inner = conv(W1[n].reshape(9 * full, full), jnp.concatenate(state, axis=1),
                         rows + 2 * edge, biases[1 + n])
            inner = inside([jnp.maximum(v, 0.0) for v in inner], 1 - edge)
            added = conv(W2[n].reshape(9 * full, full), jnp.concatenate(inner, axis=1),
                         rows + 2 * edge - 2, biases[1 + blocks + n])
            state = inside([s.astype(jnp.float32) + v for s, v in zip(state[2:-2], added)],
                           2 - edge)
            edge -= 2
        for r in range(rows):
            H[t, reach + r] = state[r]
        if t < frames - 1:
            for step in (-2, 2, -1, 1):
                @pl.when(has(step))
                def _():
                    h_copy(t, step).start()
        for k in range(chans):
            @pl.when(not_me(t, k))
            def _():
                o_copy(t, k, shot, shot).start()

            @pl.when((x == t) & (c == k))
            def _():
                out_ref[shot] = H[t, reach:reach + rows, half_of(k), :]

    for f, k in group:
        @pl.when(not_me(f, k))
        def _():
            lr_copy(f, k, 0, x, c).wait_send()
            o_copy(0, 0, f * chans + k, f * chans + k).wait_recv()
        for step in (-1, 1):
            @pl.when(has(step))
            def _():
                lr_copy(f, k, step, x, c).wait_send()
    for k in range(chans):
        @pl.when(c != k)
        def _():
            for copy in w_copies(k, c):
                copy.wait_send()
    for step in (-1, 1):
        @pl.when(has(step))
        def _():
            fl_copy(step).wait_send()
    for t in range(frames):
        if t < frames - 1:
            for step in (-1, 1, -2, 2):
                @pl.when(has(step))
                def _():
                    h_copy(t, step).wait_send()
        for k in range(chans):
            @pl.when(not_me(t, k))
            def _():
                o_copy(t, k, shot, shot).wait_send()


def by_shots(lr_feats, flow_prev, flow_second, w_join, b_join, w_first, b_first, w_second, b_second):
    shots, _, half, rows, cols = lr_feats.shape
    frames = lax.axis_size("frames")
    chans = lax.axis_size("chan")
    tiles = lax.axis_size("tiles")
    blocks = w_first.shape[0]
    halo = 1 + 2 * blocks
    reach = rows + halo
    full = half * chans
    lr = jnp.swapaxes(lr_feats[:, 0], 1, 2)
    offsets = [jnp.transpose(f[:, :, 0], (1, 2, 0)).reshape(2 * frames, shots) for f in (flow_prev, flow_second)]
    lines = -(-(1 + 2 * blocks) // 8) * 8
    kind = lr.dtype
    dma = pltpu.SemaphoreType.DMA
    out = pl.pallas_call(
        functools.partial(plain_kernel, (frames, chans, tiles, rows, half, cols, blocks)),
        out_shape=jax.ShapeDtypeStruct((shots, rows, half, cols), kind),
        in_specs=[pl.BlockSpec(memory_space=pltpu.VMEM)] * 9,
        out_specs=pl.BlockSpec(memory_space=pltpu.VMEM),
        scratch_shapes=[
            pltpu.VMEM((frames, rows + 2 * halo, full, cols), kind),
            pltpu.VMEM((frames, rows + 2 * reach, full, cols), kind),
            pltpu.VMEM((rows + 2 * reach, full, cols), kind),
            pltpu.VMEM((2, 2 * frames, 128), jnp.int32),
            pltpu.VMEM((3, 2, 2 * frames, 128), jnp.int32),
            pltpu.SMEM((3, 2, 2 * frames, 128), jnp.int32),
            pltpu.VMEM((9, full, 3 * full), kind),
            pltpu.VMEM((blocks, 9, full, full), kind),
            pltpu.VMEM((blocks, 9, full, full), kind),
            pltpu.VMEM((lines, 128), jnp.float32),
            pltpu.VMEM((chans, lines, 128), jnp.float32),
            dma((frames, chans, 3)), dma((frames, chans, 3)), dma((3,)), dma((3,)), dma,
            dma((chans, 4)), dma((chans, 4)), dma((frames, 5)), dma((frames, 5)),
            dma((frames, chans)), dma((shots,)),
        ],
        compiler_params=pltpu.CompilerParams(
            collective_id=0, has_side_effects=True, vmem_limit_bytes=40 * 1024 * 1024
        ),
    )(lr, *offsets, w_join, w_first, w_second, b_join[None], b_first, b_second)
    return jnp.swapaxes(out, 1, 2)[:, None]


def one_shot_each(lr_feats, flow_prev, flow_second, w_join, b_join, w_first, *rest):
    halo = 1 + 2 * w_first.shape[0]
    rows = lr_feats.shape[3]
    shots = lax.axis_size("frames") * lax.axis_size("chan")
    fits = (
        lr_feats.shape[0] == shots
        and flow_prev.shape[1] == lax.axis_size("frames")
        and flow_prev.shape[2] == 1
        and halo <= rows
        and lr_feats.shape[4] == 128
        and lr_feats.shape[2] <= 128
        and lr_feats.shape[0] <= 128
    )
    plan = by_shots if fits else shards
    return plan(lr_feats, flow_prev, flow_second, w_join, b_join, w_first, *rest)


def solution(mesh):
    in_specs = (
        P("clips", "frames", "chan", "tiles", None),
        P("clips", None, "tiles", None),
        P("clips", None, "tiles", None),
        P(None, "chan", None),
        P("chan"),
        P(None, None, "chan", None),
        P(None, "chan"),
        P(None, None, "chan", None),
        P(None, "chan"),
    )
    out_specs = P("clips", "frames", "chan", "tiles", None)
    return jax.shard_map(one_shot_each, mesh=mesh, in_specs=in_specs, out_specs=out_specs, check_vma=False)
```

```python
import functools

import jax
import jax.numpy as jnp
from jax import lax
from jax.experimental import pallas as pl
from jax.experimental.pallas import tpu as pltpu
from jax.sharding import PartitionSpec as P

BH = 8


def padded_2(array, sides, width):
    for axis, dim in sides:
        devices, length = (lax.axis_size(axis), array.shape[dim])
        up = [(i, (i + 1) % devices) for i in range(devices - 1)]
        down = [(j, i) for i, j in up]
        last = lax.slice_in_dim(array, length - width, length, axis=dim)
        first = lax.slice_in_dim(array, 0, width, axis=dim)
        before = lax.ppermute(last, axis, up)
        after = lax.ppermute(first, axis, down)
        array = jnp.concatenate([before, array, after], axis=dim)
    return array


def for_sending(array):
    return jax.tree.map(lambda a: a.astype(jnp.bfloat16) if a.dtype == jnp.float32 else a, array)


def shifted(block, axis, distance):
    devices = range(lax.axis_size(axis))
    route = [(i - distance, i) for i in devices if i - distance in devices]
    return lax.ppermute(block, axis, route)


def displace(rimmed, offsets, tile_rows):
    channels = rimmed.shape[0]
    col_count = rimmed.shape[2]
    padded = jnp.pad(rimmed, ((0, 0), (0, 0), (tile_rows, tile_rows)))
    start_row = tile_rows + offsets[0, 0]
    start_col = tile_rows + offsets[0, 1]
    pieces = [lax.dynamic_slice(padded, (0, start_row, start_col), (channels, BH, col_count))]
    return jnp.concatenate(pieces, axis=1)


def convolve_rows(inputs, weights, bias_vec):
    in_count, row_count, col_count = inputs.shape
    rimmed = padded_2(inputs, (("tiles", 1),), 1)
    padded = jnp.pad(rimmed, ((0, 0), (0, 0), (1, 1)))
    total_sum = jnp.zeros((weights.shape[1], row_count * col_count), jnp.float32)
    for tap_index in range(9):
        tap_row = tap_index // 3
        tap_col = tap_index % 3
        window = padded[:, tap_row : tap_row + row_count, tap_col : tap_col + col_count].reshape(
            in_count, row_count * col_count
        )
        total_sum = total_sum + jnp.dot(
            weights[tap_index], window, preferred_element_type=jnp.float32
        )
    return total_sum.reshape(-1, row_count, col_count) + bias_vec[:, None, None]


def block_conv(own_part, weights, bias_vec):
    whole_input = lax.all_gather(own_part, "chan", axis=0, tiled=True)
    return convolve_rows(whole_input, weights, bias_vec)


def refine(current, warped_one, warped_two, w_join, b_join, w_first, b_first, w_second, b_second):
    full_current, full_one, full_two = (
        lax.all_gather(current, "chan", axis=0, tiled=True),
        lax.all_gather(warped_one, "chan", axis=0, tiled=True),
        lax.all_gather(warped_two, "chan", axis=0, tiled=True),
    )
    stacked = jnp.concatenate([full_current, full_one, full_two], axis=0)
    joined_sum = convolve_rows(stacked, w_join, b_join)
    joined_state = jnp.where(joined_sum > 0, joined_sum, 0.1 * joined_sum).astype(jnp.bfloat16)
    inner_act = jnp.maximum(block_conv(joined_state, w_first[0], b_first[0]), 0.0).astype(
        jnp.bfloat16
    )
    joined_state = (
        joined_state.astype(jnp.float32) + block_conv(inner_act, w_second[0], b_second[0])
    ).astype(jnp.bfloat16)
    return joined_state


def shards(lr_feats, flow_prev, flow_second, w_join, b_join, w_first, b_first, w_second, b_second):
    segments = lr_feats.shape[0]
    tile_rows = lr_feats.shape[3]
    frames_all = flow_prev.shape[1]
    owners = lax.axis_size("frames")
    position = lax.axis_index("frames")
    blank_feat = jnp.zeros(lr_feats.shape[2:], lr_feats.dtype)

    def advance(turn_index, carried):
        results, first_in, second_in, second_wait = carried
        segment = turn_index - position
        is_valid = (segment >= 0) & (segment < segments)
        seg_clip = jnp.clip(segment, 0, segments - 1)
        current = lax.dynamic_index_in_dim(lr_feats, seg_clip, 0, keepdims=False)[0]
        fresh_state = refine(
            current, first_in, second_in, w_join, b_join, w_first, b_first, w_second, b_second
        )
        kept_slice = lax.dynamic_index_in_dim(results, seg_clip, 0, keepdims=True)
        chosen = jnp.where(is_valid, fresh_state[None, None], kept_slice)
        results = lax.dynamic_update_index_in_dim(results, chosen[0], seg_clip, 0)
        rimmed_own = padded_2(fresh_state, (("tiles", 1),), tile_rows)
        frame_next = jnp.minimum(position + 1, frames_all - 1)
        frame_after = jnp.minimum(position + 2, frames_all - 1)
        ahead_one = displace(rimmed_own, flow_prev[seg_clip, frame_next], tile_rows)
        ahead_two = displace(rimmed_own, flow_second[seg_clip, frame_after], tile_rows)
        first_next = shifted(for_sending(ahead_one), "frames", 1).astype(ahead_one.dtype)
        wait_next = shifted(for_sending(ahead_two), "frames", 2).astype(ahead_two.dtype)
        return (results, first_next, second_wait, wait_next)

    initial = (jnp.zeros_like(lr_feats), blank_feat, blank_feat, blank_feat)
    results, first_in, second_in, second_wait = lax.fori_loop(
        0, segments + owners - 1, advance, initial
    )
    return results


MESH = pl.DeviceIdType.MESH


def plain_kernel(
    sizes,
    lr_in, fp_in, fs_in, wj_ref, w1_ref, w2_ref, bj_in, b1_in, b2_in,
    out_ref,
    lr_got, lr_ref, fp_ref, fs_ref, bj_ref, b1_ref, b2_ref, in_sem,
    L, H, blank, FA, FL, FS, WJ, W1, W2, BA, B,
    lr_send, lr_recv, fl_send, fl_recv, fl_sem, w_send, w_recv, h_send, h_recv, o_send, o_recv,
):
    frames, chans, tiles, rows, half, cols, blocks = sizes
    halo = 1 + 2 * blocks
    reach = rows + halo
    full = half * chans
    clip = lax.axis_index("clips")
    z = lax.axis_index("tiles")
    x = lax.axis_index("frames")
    c = lax.axis_index("chan")
    shot = x * chans + c
    group = [(f, k) for f in range(frames) for k in range(chans)]

    def has(step):
        return (z + step >= 0) & (z + step < tiles)

    def not_me(f, k):
        return jnp.logical_not((x == f) & (c == k))

    def half_of(k):
        return pl.ds(k * half if isinstance(k, int) else pl.multiple_of(k * half, half), half)

    def remote(src, dst, send, recv, dev):
        return pltpu.make_async_remote_copy(
            src_ref=src, dst_ref=dst, send_sem=send, recv_sem=recv,
            device_id=(clip,) + dev, device_id_type=MESH,
        )

    moves = [(lr_in, lr_got), (fp_in, fp_ref), (fs_in, fs_ref), (bj_in, bj_ref), (b1_in, b1_ref),
             (b2_in, b2_ref), (wj_ref, WJ.at[:, half_of(c)]), (w1_ref, W1.at[:, :, half_of(c)]),
             (w2_ref, W2.at[:, :, half_of(c)])]
    moves = [pltpu.make_async_copy(a, b, in_sem.at[n]) for n, (a, b) in enumerate(moves)]
    loads, own_weights = moves[:6], moves[6:]
    for copy in moves:
        copy.start()

    for f in range(frames):
        for part in (slice(0, halo), slice(halo + rows, 2 * halo + rows)):
            L[f, part] = jnp.zeros((halo, full, cols), L.dtype)
        for part in (slice(0, reach), slice(reach + rows, 2 * reach + rows)):
            H[f, part] = jnp.zeros((reach, full, cols), H.dtype)
    FL[...] = jnp.zeros(FL.shape, FL.dtype)
    FA[...] = jnp.zeros(FA.shape, FA.dtype)
    BA[...] = jnp.zeros(BA.shape, BA.dtype)

    barrier = pltpu.get_barrier_semaphore()

    def greet(dev):
        pl.semaphore_signal(barrier, inc=1, device_id=(clip,) + dev, device_id_type=MESH)

    count = len(group) - 1
    for f, k in group:
        @pl.when(not_me(f, k))
        def _():
            greet((z, f, k))
    for step in (-1, 1):
        for f, k in group:
            @pl.when(has(step))
            def _():
                greet((z + step, f, k))
        count = count + jnp.where(has(step), len(group), 0)
    for step in (-2, 2):
        @pl.when(has(step))
        def _():
            greet((z + step, x, c))
        count = count + jnp.where(has(step), 1, 0)
    for copy in loads:
        copy.wait()
    FA[0, :, 0:frames * chans] = fp_ref[...]
    FA[1, :, 0:frames * chans] = fs_ref[...]
    for n, ref in enumerate([bj_ref] + [b1_ref.at[m:m + 1] for m in range(blocks)] + [b2_ref.at[m:m + 1] for m in range(blocks)]):
        BA[n:n + 1, 0:half] = ref[...]
    for s in range(frames * chans):
        turned = jnp.swapaxes(lr_got[s, 0].astype(jnp.float32), 0, 1)
        lr_ref[s] = turned.astype(lr_ref.dtype)
    L[x, halo:halo + rows, half_of(c), :] = lr_ref[shot]
    B[c] = BA[...]
    FL[1] = FA[...]
    blank[...] = jnp.zeros(blank.shape, blank.dtype)
    pl.semaphore_wait(barrier, count)

    span = {0: (0, rows, halo), 1: (rows - halo, halo, 0), -1: (0, halo, halo + rows)}

    def lr_copy(f, k, step, src_f, src_k):
        start, length, land = span[step]
        return remote(
            lr_ref.at[f * chans + k, pl.ds(start, length)],
            L.at[src_f, pl.ds(land, length), half_of(src_k)],
            lr_send.at[f, k, step + 1], lr_recv.at[src_f, src_k, step + 1],
            (z + step, f, k),
        )

    def w_copies(k, src_k):
        pairs = [(wj_ref, WJ.at[:, half_of(src_k)]), (w1_ref, W1.at[:, :, half_of(src_k)]),
                 (w2_ref, W2.at[:, :, half_of(src_k)]), (BA, B.at[src_k])]
        return [remote(a, b, w_send.at[k, n], w_recv.at[src_k, n], (z, x, k))
                for n, (a, b) in enumerate(pairs)]

    def fl_copy(step):
        return remote(FA, FL.at[1 - step], fl_send.at[step + 1],
                      fl_recv.at[step + 1], (z + step, x, c))

    def send_lr(f, k, step):
        @pl.when(not_me(f, k) if step == 0 else has(step))
        def _():
            lr_copy(f, k, step, x, c).start()

    for step in (-1, 1):
        @pl.when(has(step))
        def _():
            fl_copy(step).start()
    for step in (0, -1, 1):
        for turn in range(frames):
            f = lax.rem(x + frames - 1 - turn, frames)
            for k in range(chans):
                send_lr(f, k, step)
        if step == 0:
            for k in range(chans):
                @pl.when(c != k)
                def _():
                    for copy in w_copies(k, c):
                        copy.start()
    for step in (-1, 1):
        @pl.when(has(-step))
        def _():
            fl_copy(step).wait_recv()
    to_scalars = pltpu.make_async_copy(FL, FS, fl_sem)
    to_scalars.start()
    to_scalars.wait()

    lane = lax.broadcasted_iota(jnp.int32, (full, cols), 1)

    def displaced(which, t):
        age = t - 1 - which
        rows_out = []
        for j in range(-halo, rows + halo):
            near = 0 if j < 0 else (1 if j < rows else 2)
            dy = FS[near, which, 2 * t, shot]
            dx = FS[near, which, 2 * t + 1, shot]
            source = reach + j + dy
            v = (H[age, source] if age >= 0 else blank[source]).astype(jnp.float32)
            turned = pltpu.roll(v, lax.rem(cols - dx, cols), 1)
            seen = lane + dx
            rows_out.append(
                jnp.where((seen >= 0) & (seen < cols), turned, 0.0).astype(jnp.bfloat16))
        return jnp.concatenate(rows_out, axis=1)

    def conv(weights, inputs, count, bias):
        y = jnp.dot(weights, inputs, preferred_element_type=jnp.float32)
        result = []
        for r in range(1, count - 1):
            sides = []
            for j in range(3):
                total = None
                for i in range(3):
                    first = (3 * i + j) * full
                    part = y[first:first + full, (r + i - 1) * cols:(r + i) * cols]
                    total = part if total is None else total + part
                sides.append(total)
            left = jnp.where(lane == 0, 0.0, pltpu.roll(sides[0], 1, 1))
            right = jnp.where(lane == cols - 1, 0.0, pltpu.roll(sides[2], cols - 1, 1))
            result.append(sides[1] + left + right + bias)
        return result

    def inside(values, first):
        kept = []
        for n, v in enumerate(values):
            j = first + n
            if j < 0:
                v = jnp.where(z > 0, v, 0.0)
            elif j >= rows:
                v = jnp.where(z < tiles - 1, v, 0.0)
            kept.append(v.astype(jnp.bfloat16))
        return kept

    def h_copy(t, step):
        start, length = (0, rows) if abs(step) == 1 else ((rows - halo, halo) if step > 0 else (0, halo))
        return remote(
            H.at[t, pl.ds(reach + start, length)],
            H.at[t, pl.ds(reach + start - step * rows, length)],
            h_send.at[t, step + 2], h_recv.at[t, step + 2], (z + step, x, c),
        )

    def o_copy(t, k, to_shot, src):
        return remote(H.at[t, pl.ds(reach, rows), half_of(k)], out_ref.at[to_shot],
                      o_send.at[t, k], o_recv.at[src], (z, t, k))

    corner = lax.broadcasted_iota(jnp.int32, (half, 128), 0) == lax.broadcasted_iota(
        jnp.int32, (half, 128), 1)

    def bias_of(n):
        parts = [jnp.sum(jnp.where(corner, B[k, n:n + 1, :], 0.0), axis=1, keepdims=True)
                 for k in range(chans)]
        return jnp.broadcast_to(jnp.concatenate(parts, axis=0), (full, cols))

    for t in range(frames):
        warped_two = displaced(1, t)
        if t == 0:
            warped_one = displaced(0, t)
            for k in range(chans):
                @pl.when(c != k)
                def _():
                    for copy in w_copies(c, k):
                        copy.wait_recv()
            for copy in own_weights:
                copy.wait()
            biases = [bias_of(n) for n in range(1 + 2 * blocks)]
        for k in range(chans):
            @pl.when(not_me(t, k))
            def _():
                lr_copy(x, c, 0, t, k).wait_recv()
            for step in (-1, 1):
                @pl.when(has(-step))
                def _():
                    lr_copy(x, c, step, t, k).wait_recv()
        if t > 0:
            for step in (-2, -1, 1, 2):
                @pl.when(has(-step))
                def _():
                    h_copy(t - 1, step).wait_recv()
            warped_one = displaced(0, t)
        current = jnp.concatenate([L[t, r] for r in range(rows + 2 * halo)], axis=1)
        stacked = jnp.concatenate([current, warped_one, warped_two], axis=0)
        edge = halo - 1
        joined = conv(WJ[...].reshape(9 * full, 3 * full), stacked, rows + 2 * halo, biases[0])
        state = inside([jnp.maximum(v, 0.1 * v) for v in joined], -edge)
        for n in range(blocks):
            inner = conv(W1[n].reshape(9 * full, full), jnp.concatenate(state, axis=1),
                         rows + 2 * edge, biases[1 + n])
            inner = inside([jnp.maximum(v, 0.0) for v in inner], 1 - edge)
            added = conv(W2[n].reshape(9 * full, full), jnp.concatenate(inner, axis=1),
                         rows + 2 * edge - 2, biases[1 + blocks + n])
            state = inside([s.astype(jnp.float32) + v for s, v in zip(state[2:-2], added)],
                           2 - edge)
            edge -= 2
        for r in range(rows):
            H[t, reach + r] = state[r]
        if t < frames - 1:
            for step in (-2, 2, -1, 1):
                @pl.when(has(step))
                def _():
                    h_copy(t, step).start()
        for k in range(chans):
            @pl.when(not_me(t, k))
            def _():
                o_copy(t, k, shot, shot).start()

            @pl.when((x == t) & (c == k))
            def _():
                out_ref[shot] = H[t, reach:reach + rows, half_of(k), :]

    for f, k in group:
        @pl.when(not_me(f, k))
        def _():
            lr_copy(f, k, 0, x, c).wait_send()
            o_copy(0, 0, f * chans + k, f * chans + k).wait_recv()
        for step in (-1, 1):
            @pl.when(has(step))
            def _():
                lr_copy(f, k, step, x, c).wait_send()
    for k in range(chans):
        @pl.when(c != k)
        def _():
            for copy in w_copies(k, c):
                copy.wait_send()
    for step in (-1, 1):
        @pl.when(has(step))
        def _():
            fl_copy(step).wait_send()
    for t in range(frames):
        if t < frames - 1:
            for step in (-1, 1, -2, 2):
                @pl.when(has(step))
                def _():
                    h_copy(t, step).wait_send()
        for k in range(chans):
            @pl.when(not_me(t, k))
            def _():
                o_copy(t, k, shot, shot).wait_send()


def by_shots(lr_feats, flow_prev, flow_second, w_join, b_join, w_first, b_first, w_second, b_second):
    shots, _, half, rows, cols = lr_feats.shape
    frames = lax.axis_size("frames")
    chans = lax.axis_size("chan")
    tiles = lax.axis_size("tiles")
    blocks = w_first.shape[0]
    halo = 1 + 2 * blocks
    reach = rows + halo
    full = half * chans
    offsets = [jnp.transpose(f[:, :, 0], (1, 2, 0)).reshape(2 * frames, shots) for f in (flow_prev, flow_second)]
    lines = -(-(1 + 2 * blocks) // 8) * 8
    kind = lr_feats.dtype
    own_bias = (blocks, half)
    dma = pltpu.SemaphoreType.DMA
    out = pl.pallas_call(
        functools.partial(plain_kernel, (frames, chans, tiles, rows, half, cols, blocks)),
        out_shape=jax.ShapeDtypeStruct((shots, rows, half, cols), kind),
        in_specs=[pl.BlockSpec(memory_space=pltpu.HBM)] * 9,
        out_specs=pl.BlockSpec(memory_space=pltpu.VMEM),
        scratch_shapes=[
            pltpu.VMEM(lr_feats.shape, kind),
            pltpu.VMEM((shots, rows, half, cols), kind),
            pltpu.VMEM((2 * frames, shots), jnp.int32),
            pltpu.VMEM((2 * frames, shots), jnp.int32),
            pltpu.VMEM((1, half), jnp.float32),
            pltpu.VMEM(own_bias, jnp.float32),
            pltpu.VMEM(own_bias, jnp.float32),
            dma((9,)),
            pltpu.VMEM((frames, rows + 2 * halo, full, cols), kind),
            pltpu.VMEM((frames, rows + 2 * reach, full, cols), kind),
            pltpu.VMEM((rows + 2 * reach, full, cols), kind),
            pltpu.VMEM((2, 2 * frames, 128), jnp.int32),
            pltpu.VMEM((3, 2, 2 * frames, 128), jnp.int32),
            pltpu.SMEM((3, 2, 2 * frames, 128), jnp.int32),
            pltpu.VMEM((9, full, 3 * full), kind),
            pltpu.VMEM((blocks, 9, full, full), kind),
            pltpu.VMEM((blocks, 9, full, full), kind),
            pltpu.VMEM((lines, 128), jnp.float32),
            pltpu.VMEM((chans, lines, 128), jnp.float32),
            dma((frames, chans, 3)), dma((frames, chans, 3)), dma((3,)), dma((3,)), dma,
            dma((chans, 4)), dma((chans, 4)), dma((frames, 5)), dma((frames, 5)),
            dma((frames, chans)), dma((shots,)),
        ],
        compiler_params=pltpu.CompilerParams(
            collective_id=0, has_side_effects=True, vmem_limit_bytes=64 * 1024 * 1024
        ),
    )(lr_feats, *offsets, w_join, w_first, w_second, b_join[None], b_first, b_second)
    return jnp.swapaxes(out, 1, 2)[:, None]


def one_shot_each(lr_feats, flow_prev, flow_second, w_join, b_join, w_first, *rest):
    halo = 1 + 2 * w_first.shape[0]
    rows = lr_feats.shape[3]
    shots = lax.axis_size("frames") * lax.axis_size("chan")
    fits = (
        lr_feats.shape[0] == shots
        and flow_prev.shape[1] == lax.axis_size("frames")
        and flow_prev.shape[2] == 1
        and halo <= rows
        and lr_feats.shape[4] == 128
        and lr_feats.shape[2] <= 128
        and lr_feats.shape[0] <= 128
    )
    plan = by_shots if fits else shards
    return plan(lr_feats, flow_prev, flow_second, w_join, b_join, w_first, *rest)


def solution(mesh):
    in_specs = (
        P("clips", "frames", "chan", "tiles", None),
        P("clips", None, "tiles", None),
        P("clips", None, "tiles", None),
        P(None, "chan", None),
        P("chan"),
        P(None, None, "chan", None),
        P(None, "chan"),
        P(None, None, "chan", None),
        P(None, "chan"),
    )
    out_specs = P("clips", "frames", "chan", "tiles", None)
    return jax.shard_map(one_shot_each, mesh=mesh, in_specs=in_specs, out_specs=out_specs, check_vma=False)
```

```python
import functools

import jax
import jax.numpy as jnp
from jax import lax
from jax.experimental import pallas as pl
from jax.experimental.pallas import tpu as pltpu
from jax.sharding import PartitionSpec as P

BH = 8


def padded_2(array, sides, width):
    for axis, dim in sides:
        devices, length = (lax.axis_size(axis), array.shape[dim])
        up = [(i, (i + 1) % devices) for i in range(devices - 1)]
        down = [(j, i) for i, j in up]
        last = lax.slice_in_dim(array, length - width, length, axis=dim)
        first = lax.slice_in_dim(array, 0, width, axis=dim)
        before = lax.ppermute(last, axis, up)
        after = lax.ppermute(first, axis, down)
        array = jnp.concatenate([before, array, after], axis=dim)
    return array


def for_sending(array):
    return jax.tree.map(lambda a: a.astype(jnp.bfloat16) if a.dtype == jnp.float32 else a, array)


def shifted(block, axis, distance):
    devices = range(lax.axis_size(axis))
    route = [(i - distance, i) for i in devices if i - distance in devices]
    return lax.ppermute(block, axis, route)


def displace(rimmed, offsets, tile_rows):
    channels = rimmed.shape[0]
    col_count = rimmed.shape[2]
    padded = jnp.pad(rimmed, ((0, 0), (0, 0), (tile_rows, tile_rows)))
    start_row = tile_rows + offsets[0, 0]
    start_col = tile_rows + offsets[0, 1]
    pieces = [lax.dynamic_slice(padded, (0, start_row, start_col), (channels, BH, col_count))]
    return jnp.concatenate(pieces, axis=1)


def convolve_rows(inputs, weights, bias_vec):
    in_count, row_count, col_count = inputs.shape
    rimmed = padded_2(inputs, (("tiles", 1),), 1)
    padded = jnp.pad(rimmed, ((0, 0), (0, 0), (1, 1)))
    total_sum = jnp.zeros((weights.shape[1], row_count * col_count), jnp.float32)
    for tap_index in range(9):
        tap_row = tap_index // 3
        tap_col = tap_index % 3
        window = padded[:, tap_row : tap_row + row_count, tap_col : tap_col + col_count].reshape(
            in_count, row_count * col_count
        )
        total_sum = total_sum + jnp.dot(
            weights[tap_index], window, preferred_element_type=jnp.float32
        )
    return total_sum.reshape(-1, row_count, col_count) + bias_vec[:, None, None]


def block_conv(own_part, weights, bias_vec):
    whole_input = lax.all_gather(own_part, "chan", axis=0, tiled=True)
    return convolve_rows(whole_input, weights, bias_vec)


def refine(current, warped_one, warped_two, w_join, b_join, w_first, b_first, w_second, b_second):
    full_current, full_one, full_two = (
        lax.all_gather(current, "chan", axis=0, tiled=True),
        lax.all_gather(warped_one, "chan", axis=0, tiled=True),
        lax.all_gather(warped_two, "chan", axis=0, tiled=True),
    )
    stacked = jnp.concatenate([full_current, full_one, full_two], axis=0)
    joined_sum = convolve_rows(stacked, w_join, b_join)
    joined_state = jnp.where(joined_sum > 0, joined_sum, 0.1 * joined_sum).astype(jnp.bfloat16)
    inner_act = jnp.maximum(block_conv(joined_state, w_first[0], b_first[0]), 0.0).astype(
        jnp.bfloat16
    )
    joined_state = (
        joined_state.astype(jnp.float32) + block_conv(inner_act, w_second[0], b_second[0])
    ).astype(jnp.bfloat16)
    return joined_state


def shards(lr_feats, flow_prev, flow_second, w_join, b_join, w_first, b_first, w_second, b_second):
    segments = lr_feats.shape[0]
    tile_rows = lr_feats.shape[3]
    frames_all = flow_prev.shape[1]
    owners = lax.axis_size("frames")
    position = lax.axis_index("frames")
    blank_feat = jnp.zeros(lr_feats.shape[2:], lr_feats.dtype)

    def advance(turn_index, carried):
        results, first_in, second_in, second_wait = carried
        segment = turn_index - position
        is_valid = (segment >= 0) & (segment < segments)
        seg_clip = jnp.clip(segment, 0, segments - 1)
        current = lax.dynamic_index_in_dim(lr_feats, seg_clip, 0, keepdims=False)[0]
        fresh_state = refine(
            current, first_in, second_in, w_join, b_join, w_first, b_first, w_second, b_second
        )
        kept_slice = lax.dynamic_index_in_dim(results, seg_clip, 0, keepdims=True)
        chosen = jnp.where(is_valid, fresh_state[None, None], kept_slice)
        results = lax.dynamic_update_index_in_dim(results, chosen[0], seg_clip, 0)
        rimmed_own = padded_2(fresh_state, (("tiles", 1),), tile_rows)
        frame_next = jnp.minimum(position + 1, frames_all - 1)
        frame_after = jnp.minimum(position + 2, frames_all - 1)
        ahead_one = displace(rimmed_own, flow_prev[seg_clip, frame_next], tile_rows)
        ahead_two = displace(rimmed_own, flow_second[seg_clip, frame_after], tile_rows)
        first_next = shifted(for_sending(ahead_one), "frames", 1).astype(ahead_one.dtype)
        wait_next = shifted(for_sending(ahead_two), "frames", 2).astype(ahead_two.dtype)
        return (results, first_next, second_wait, wait_next)

    initial = (jnp.zeros_like(lr_feats), blank_feat, blank_feat, blank_feat)
    results, first_in, second_in, second_wait = lax.fori_loop(
        0, segments + owners - 1, advance, initial
    )
    return results


MESH = pl.DeviceIdType.MESH


def plain_kernel(
    sizes,
    lr_in, fp_in, fs_in, wj_ref, w1_ref, w2_ref, bj_in, b1_in, b2_in,
    out_ref,
    lr_got, lr_ref, fp_ref, fs_ref, bj_ref, b1_ref, b2_ref, in_sem,
    L, H, blank, FA, FL, FS, WJ, W1, W2, BA, B,
    lr_send, lr_recv, fl_send, fl_recv, fl_sem, w_send, w_recv, h_send, h_recv, o_send, o_recv,
):
    frames, chans, tiles, rows, half, cols, blocks = sizes
    halo = 1 + 2 * blocks
    reach = rows + halo
    full = half * chans
    clip = lax.axis_index("clips")
    z = lax.axis_index("tiles")
    x = lax.axis_index("frames")
    c = lax.axis_index("chan")
    shot = x * chans + c
    group = [(f, k) for f in range(frames) for k in range(chans)]

    def has(step):
        return (z + step >= 0) & (z + step < tiles)

    def not_me(f, k):
        return jnp.logical_not((x == f) & (c == k))

    def half_of(k):
        return pl.ds(k * half if isinstance(k, int) else pl.multiple_of(k * half, half), half)

    def remote(src, dst, send, recv, dev):
        return pltpu.make_async_remote_copy(
            src_ref=src, dst_ref=dst, send_sem=send, recv_sem=recv,
            device_id=(clip,) + dev, device_id_type=MESH,
        )

    moves = [(lr_in, lr_got), (fp_in, fp_ref), (fs_in, fs_ref), (bj_in, bj_ref), (b1_in, b1_ref),
             (b2_in, b2_ref), (wj_ref, WJ.at[:, half_of(c)]), (w1_ref, W1.at[:, :, half_of(c)]),
             (w2_ref, W2.at[:, :, half_of(c)])]
    moves = [pltpu.make_async_copy(a, b, in_sem.at[n]) for n, (a, b) in enumerate(moves)]
    loads, own_weights = moves[:6], moves[6:]
    for copy in moves:
        copy.start()

    for f in range(frames):
        for part in (slice(0, halo), slice(halo + rows, 2 * halo + rows)):
            L[f, part] = jnp.zeros((halo, full, cols), L.dtype)
        for part in (slice(0, reach), slice(reach + rows, 2 * reach + rows)):
            H[f, part] = jnp.zeros((reach, full, cols), H.dtype)
    FL[...] = jnp.zeros(FL.shape, FL.dtype)
    FA[...] = jnp.zeros(FA.shape, FA.dtype)
    BA[...] = jnp.zeros(BA.shape, BA.dtype)

    barrier = pltpu.get_barrier_semaphore()

    def greet(dev):
        pl.semaphore_signal(barrier, inc=1, device_id=(clip,) + dev, device_id_type=MESH)

    count = len(group) - 1
    for f, k in group:
        @pl.when(not_me(f, k))
        def _():
            greet((z, f, k))
    for step in (-1, 1):
        for f, k in group:
            @pl.when(has(step))
            def _():
                greet((z + step, f, k))
        count = count + jnp.where(has(step), len(group), 0)
    for step in (-2, 2):
        @pl.when(has(step))
        def _():
            greet((z + step, x, c))
        count = count + jnp.where(has(step), 1, 0)
    for copy in loads:
        copy.wait()
    FA[0, :, 0:frames * chans] = fp_ref[...]
    FA[1, :, 0:frames * chans] = fs_ref[...]
    for n, ref in enumerate([bj_ref] + [b1_ref.at[m:m + 1] for m in range(blocks)] + [b2_ref.at[m:m + 1] for m in range(blocks)]):
        BA[n:n + 1, 0:half] = ref[...]
    for s in range(frames * chans):
        turned = jnp.swapaxes(lr_got[s, 0].astype(jnp.float32), 0, 1)
        lr_ref[s] = turned.astype(lr_ref.dtype)
    L[x, halo:halo + rows, half_of(c), :] = lr_ref[shot]
    B[c] = BA[...]
    FL[1] = FA[...]
    blank[...] = jnp.zeros(blank.shape, blank.dtype)
    pl.semaphore_wait(barrier, count)

    span = {0: (0, rows, halo), 1: (rows - halo, halo, 0), -1: (0, halo, halo + rows)}

    def lr_copy(f, k, step, src_f, src_k):
        start, length, land = span[step]
        return remote(
            lr_ref.at[f * chans + k, pl.ds(start, length)],
            L.at[src_f, pl.ds(land, length), half_of(src_k)],
            lr_send.at[f, k, step + 1], lr_recv.at[src_f, src_k, step + 1],
            (z + step, f, k),
        )

    def w_copies(k, src_k):
        pairs = [(wj_ref, WJ.at[:, half_of(src_k)]), (w1_ref, W1.at[:, :, half_of(src_k)]),
                 (w2_ref, W2.at[:, :, half_of(src_k)]), (BA, B.at[src_k])]
        return [remote(a, b, w_send.at[k, n], w_recv.at[src_k, n], (z, x, k))
                for n, (a, b) in enumerate(pairs)]

    def fl_copy(step):
        return remote(FA, FL.at[1 - step], fl_send.at[step + 1],
                      fl_recv.at[step + 1], (z + step, x, c))

    def send_lr(f, k, step):
        @pl.when(not_me(f, k) if step == 0 else has(step))
        def _():
            lr_copy(f, k, step, x, c).start()

    for step in (-1, 1):
        @pl.when(has(step))
        def _():
            fl_copy(step).start()
    for step in (0, -1, 1):
        for turn in range(frames):
            f = lax.rem(x + frames - 1 - turn, frames)
            for k in range(chans):
                send_lr(f, k, step)
        if step == 0:
            for k in range(chans):
                @pl.when(c != k)
                def _():
                    for copy in w_copies(k, c):
                        copy.start()
    for step in (-1, 1):
        @pl.when(has(-step))
        def _():
            fl_copy(step).wait_recv()
    to_scalars = pltpu.make_async_copy(FL, FS, fl_sem)
    to_scalars.start()
    to_scalars.wait()

    lane = lax.broadcasted_iota(jnp.int32, (full, cols), 1)

    def displaced(which, t):
        age = t - 1 - which
        rows_out = []
        for j in range(-halo, rows + halo):
            near = 0 if j < 0 else (1 if j < rows else 2)
            dy = FS[near, which, 2 * t, shot]
            dx = FS[near, which, 2 * t + 1, shot]
            source = reach + j + dy
            v = (H[age, source] if age >= 0 else blank[source]).astype(jnp.float32)
            turned = pltpu.roll(v, lax.rem(cols - dx, cols), 1)
            seen = lane + dx
            rows_out.append(
                jnp.where((seen >= 0) & (seen < cols), turned, 0.0).astype(jnp.bfloat16))
        return jnp.concatenate(rows_out, axis=1)

    def conv(weights, inputs, count, bias):
        y = jnp.dot(weights, inputs, preferred_element_type=jnp.float32)
        result = []
        for r in range(1, count - 1):
            sides = []
            for j in range(3):
                total = None
                for i in range(3):
                    first = (3 * i + j) * full
                    part = y[first:first + full, (r + i - 1) * cols:(r + i) * cols]
                    total = part if total is None else total + part
                sides.append(total)
            left = jnp.where(lane == 0, 0.0, pltpu.roll(sides[0], 1, 1))
            right = jnp.where(lane == cols - 1, 0.0, pltpu.roll(sides[2], cols - 1, 1))
            result.append(sides[1] + left + right + bias)
        return result

    def inside(values, first):
        kept = []
        for n, v in enumerate(values):
            j = first + n
            if j < 0:
                v = jnp.where(z > 0, v, 0.0)
            elif j >= rows:
                v = jnp.where(z < tiles - 1, v, 0.0)
            kept.append(v.astype(jnp.bfloat16))
        return kept

    def h_copy(t, step):
        start, length = (0, rows) if abs(step) == 1 else ((rows - halo, halo) if step > 0 else (0, halo))
        return remote(
            H.at[t, pl.ds(reach + start, length)],
            H.at[t, pl.ds(reach + start - step * rows, length)],
            h_send.at[t, step + 2], h_recv.at[t, step + 2], (z + step, x, c),
        )

    def o_copy(t, k, to_shot, src):
        return remote(H.at[t, pl.ds(reach, rows), half_of(k)], out_ref.at[to_shot],
                      o_send.at[t, k], o_recv.at[src], (z, t, k))

    corner = lax.broadcasted_iota(jnp.int32, (half, 128), 0) == lax.broadcasted_iota(
        jnp.int32, (half, 128), 1)

    def bias_of(n):
        parts = [jnp.sum(jnp.where(corner, B[k, n:n + 1, :], 0.0), axis=1, keepdims=True)
                 for k in range(chans)]
        return jnp.broadcast_to(jnp.concatenate(parts, axis=0), (full, cols))

    for t in range(frames):
        warped_two = displaced(1, t)
        if t == 0:
            warped_one = displaced(0, t)
            for k in range(chans):
                @pl.when(c != k)
                def _():
                    for copy in w_copies(c, k):
                        copy.wait_recv()
            for copy in own_weights:
                copy.wait()
            biases = [bias_of(n) for n in range(1 + 2 * blocks)]
        for k in range(chans):
            @pl.when(not_me(t, k))
            def _():
                lr_copy(x, c, 0, t, k).wait_recv()
            for step in (-1, 1):
                @pl.when(has(-step))
                def _():
                    lr_copy(x, c, step, t, k).wait_recv()
        if t > 0:
            for step in (-2, -1, 1, 2):
                @pl.when(has(-step))
                def _():
                    h_copy(t - 1, step).wait_recv()
            warped_one = displaced(0, t)
        current = jnp.concatenate([L[t, r] for r in range(rows + 2 * halo)], axis=1)
        stacked = jnp.concatenate([current, warped_one, warped_two], axis=0)
        edge = halo - 1
        joined = conv(WJ[...].reshape(9 * full, 3 * full), stacked, rows + 2 * halo, biases[0])
        state = inside([jnp.maximum(v, 0.1 * v) for v in joined], -edge)
        for n in range(blocks):
            inner = conv(W1[n].reshape(9 * full, full), jnp.concatenate(state, axis=1),
                         rows + 2 * edge, biases[1 + n])
            inner = inside([jnp.maximum(v, 0.0) for v in inner], 1 - edge)
            added = conv(W2[n].reshape(9 * full, full), jnp.concatenate(inner, axis=1),
                         rows + 2 * edge - 2, biases[1 + blocks + n])
            state = inside([s.astype(jnp.float32) + v for s, v in zip(state[2:-2], added)],
                           2 - edge)
            edge -= 2
        for r in range(rows):
            H[t, reach + r] = state[r]
        if t < frames - 1:
            for step in (-2, 2, -1, 1):
                @pl.when(has(step))
                def _():
                    h_copy(t, step).start()
        for k in range(chans):
            @pl.when(not_me(t, k))
            def _():
                o_copy(t, k, shot, shot).start()

            @pl.when((x == t) & (c == k))
            def _():
                out_ref[shot] = H[t, reach:reach + rows, half_of(k), :]

    for f, k in group:
        @pl.when(not_me(f, k))
        def _():
            lr_copy(f, k, 0, x, c).wait_send()
            o_copy(0, 0, f * chans + k, f * chans + k).wait_recv()
        for step in (-1, 1):
            @pl.when(has(step))
            def _():
                lr_copy(f, k, step, x, c).wait_send()
    for k in range(chans):
        @pl.when(c != k)
        def _():
            for copy in w_copies(k, c):
                copy.wait_send()
    for step in (-1, 1):
        @pl.when(has(step))
        def _():
            fl_copy(step).wait_send()
    for t in range(frames):
        if t < frames - 1:
            for step in (-1, 1, -2, 2):
                @pl.when(has(step))
                def _():
                    h_copy(t, step).wait_send()
        for k in range(chans):
            @pl.when(not_me(t, k))
            def _():
                o_copy(t, k, shot, shot).wait_send()


def by_shots(lr_feats, flow_prev, flow_second, w_join, b_join, w_first, b_first, w_second, b_second):
    shots, _, half, rows, cols = lr_feats.shape
    frames = lax.axis_size("frames")
    chans = lax.axis_size("chan")
    tiles = lax.axis_size("tiles")
    blocks = w_first.shape[0]
    halo = 1 + 2 * blocks
    reach = rows + halo
    full = half * chans
    offsets = [jnp.transpose(f[:, :, 0], (1, 2, 0)).reshape(2 * frames, shots) for f in (flow_prev, flow_second)]
    lines = -(-(1 + 2 * blocks) // 8) * 8
    kind = lr_feats.dtype
    own_bias = (blocks, half)
    dma = pltpu.SemaphoreType.DMA
    out = pl.pallas_call(
        functools.partial(plain_kernel, (frames, chans, tiles, rows, half, cols, blocks)),
        out_shape=jax.ShapeDtypeStruct((shots, rows, half, cols), kind),
        in_specs=[pl.BlockSpec(memory_space=pltpu.HBM)] * 9,
        out_specs=pl.BlockSpec(memory_space=pltpu.VMEM),
        scratch_shapes=[
            pltpu.VMEM(lr_feats.shape, kind),
            pltpu.VMEM((shots, rows, half, cols), kind),
            pltpu.VMEM((2 * frames, shots), jnp.int32),
            pltpu.VMEM((2 * frames, shots), jnp.int32),
            pltpu.VMEM((1, half), jnp.float32),
            pltpu.VMEM(own_bias, jnp.float32),
            pltpu.VMEM(own_bias, jnp.float32),
            dma((9,)),
            pltpu.VMEM((frames, rows + 2 * halo, full, cols), kind),
            pltpu.VMEM((frames, rows + 2 * reach, full, cols), kind),
            pltpu.VMEM((rows + 2 * reach, full, cols), kind),
            pltpu.VMEM((2, 2 * frames, 128), jnp.int32),
            pltpu.VMEM((3, 2, 2 * frames, 128), jnp.int32),
            pltpu.SMEM((3, 2, 2 * frames, 128), jnp.int32),
            pltpu.VMEM((9, full, 3 * full), kind),
            pltpu.VMEM((blocks, 9, full, full), kind),
            pltpu.VMEM((blocks, 9, full, full), kind),
            pltpu.VMEM((lines, 128), jnp.float32),
            pltpu.VMEM((chans, lines, 128), jnp.float32),
            dma((frames, chans, 3)), dma((frames, chans, 3)), dma((3,)), dma((3,)), dma,
            dma((chans, 4)), dma((chans, 4)), dma((frames, 5)), dma((frames, 5)),
            dma((frames, chans)), dma((shots,)),
        ],
        compiler_params=pltpu.CompilerParams(
            collective_id=0, has_side_effects=True, vmem_limit_bytes=40 * 1024 * 1024
        ),
    )(*[pltpu.with_memory_space_constraint(a, pltpu.HBM) for a in (lr_feats, *offsets, w_join, w_first, w_second, b_join[None], b_first, b_second)])
    return jnp.swapaxes(out, 1, 2)[:, None]


def one_shot_each(lr_feats, flow_prev, flow_second, w_join, b_join, w_first, *rest):
    halo = 1 + 2 * w_first.shape[0]
    rows = lr_feats.shape[3]
    shots = lax.axis_size("frames") * lax.axis_size("chan")
    fits = (
        lr_feats.shape[0] == shots
        and flow_prev.shape[1] == lax.axis_size("frames")
        and flow_prev.shape[2] == 1
        and halo <= rows
        and lr_feats.shape[4] == 128
        and lr_feats.shape[2] <= 128
        and lr_feats.shape[0] <= 128
    )
    plan = by_shots if fits else shards
    return plan(lr_feats, flow_prev, flow_second, w_join, b_join, w_first, *rest)


def solution(mesh):
    in_specs = (
        P("clips", "frames", "chan", "tiles", None),
        P("clips", None, "tiles", None),
        P("clips", None, "tiles", None),
        P(None, "chan", None),
        P("chan"),
        P(None, None, "chan", None),
        P(None, "chan"),
        P(None, None, "chan", None),
        P(None, "chan"),
    )
    out_specs = P("clips", "frames", "chan", "tiles", None)
    return jax.shard_map(one_shot_each, mesh=mesh, in_specs=in_specs, out_specs=out_specs, check_vma=False)
```
